32 devices in a mesh: half: 2 (over core), dev: 16 (over z, y, x).
Axes of the slice: x: 2, y: 2, z: 4, core: 2. Of those that a mesh axis runs over, the one named last changes fastest.
Arguments:
- field_mix: float32 [32, 32], P('half'), may hold values from -1 to 1
- alm: bfloat16 [128, 2, 32, 2048], P('dev', None, 'half'), may hold values from -6 to 6
- legendre: bfloat16 [128, 2048, 16], P('dev'), may hold values from -0.125 to 0.125
- order_ids: int32 [128], replicated, may hold values from 0 to 127, each once
- fetch_list: int32 [16, 16, 2], replicated, may hold values from -1 to 31, as said below
- scan_tiles: int32 [64, 32], P('dev'), may hold values from 0 to 31, as said below
- block_tile: int32 [64, 32], P('dev'), may hold values from 0 to 31
- block_pix: int32 [64, 16384], P('dev'), may hold values from -1 to 127, as said below
- noise_kernel: float32 [64, 512], P('dev'), may hold values from -0.24 to 0.24
- scan_weight: float32 [64], P('dev'), may hold values from 0.1 to 1
Outputs:
- binned: float32 [16, 32, 4096], P('dev', 'half')
The draws below stay inside these ranges and needn't reach their ends.
Inputs may be any that keep to these rules, and one draw needn't show every extreme that they name: `fetch_list`: entry [d, e, k] is the index, among the 32 tiles of device d, of the tile that device e fetches from d in slot k, or -1 for an empty slot; the live slots of one pair come first and name distinct tiles; every device fills all 2 slots from at least one source. `scan_tiles`: entry [n, i] is a slot source 2 + k whose fetch_list[source, n div 4, k] is not -1. `block_pix`: -1 marks a flagged sample.
All inputs are finite; a program needn't handle non-finite values.
Results may differ from the reference program's by a relative error of at most 0.007.
Values may be sent and summed in bfloat16 or wider, within the bound.
A program may use at most 128 MiB of HBM per device.

```python
import math
import jax
import jax.numpy as jnp
from jax import lax

FIELDS = 32
ELLS = 2048
NPHI = 4096
TILE = 128
BLK = 512
KW = 512
CAP = 2
TPS = 32
NBLK = 32
SCAN_DEV = 4
ORDERS = 128
CYCLES = 16
SCANS = 64
TILES_DEV = 32
N_DEV = 16


def owner_plan(key):
    plan_key = jax.random.fold_in(key, 7001)
    count_key, hot_key, tile_key, order_key = jax.random.split(plan_key, 4)
    count_draw = jax.random.randint(count_key, (N_DEV, N_DEV), 0, 4)
    counts = jnp.where(count_draw == 3, CAP, jnp.minimum(count_draw, 1))
    hottest = jax.random.randint(hot_key, (N_DEV,), 0, N_DEV)
    counts = jnp.where(jnp.arange(N_DEV)[None, :] == hottest[:, None], CAP, counts)
    scores = jax.random.randint(tile_key, (N_DEV, N_DEV, TILES_DEV), 0, 1 << 20) * TILES_DEV + jnp.arange(TILES_DEV)[None, None, :]
    ranked = jnp.argsort(scores, axis=-1)[:, :, :CAP]
    live_slot = jnp.arange(CAP)[None, None, :] < counts[:, :, None]
    by_dest = jnp.where(live_slot, ranked, -1)
    fetch_table = jnp.transpose(by_dest, (1, 0, 2)).astype(jnp.int32)
    live_flat = live_slot.reshape(N_DEV, N_DEV * CAP)
    slot_total = N_DEV * CAP
    slot_iota = jnp.arange(slot_total)
    shuffle = jax.random.randint(order_key, (N_DEV, slot_total), 0, 1 << 16) * slot_total + slot_iota[None, :]
    sort_key = jnp.where(live_flat, shuffle, (1 << 16) * slot_total + slot_iota[None, :])
    used_list = jnp.argsort(sort_key, axis=-1)
    used_count = jnp.sum(live_flat.astype(jnp.int32), axis=-1)
    entry_iota = jnp.arange(SCAN_DEV * TPS)
    picked = entry_iota[None, :] % used_count[:, None]
    scan_list = jnp.take_along_axis(used_list, picked, axis=1).reshape(N_DEV * SCAN_DEV, TPS)
    return (fetch_table, scan_list.astype(jnp.int32))


def draw_fetch_list(key, part):
    return owner_plan(key)[0]


def draw_scan_tiles(key, part):
    return owner_plan(key)[1]


def draw_block_tile(key, part):
    order_key = jax.random.fold_in(key, 7003)
    scores = jax.random.randint(order_key, (SCANS, NBLK), 0, 1 << 16) * NBLK + jnp.arange(NBLK)[None, :]
    shuffled = jnp.argsort(scores, axis=-1)
    return (shuffled % TPS).astype(jnp.int32)


def draw_block_pix(key, part):
    flag_key, pixel_key = jax.random.split(jax.random.fold_in(key, 7002))
    pixels = jax.random.randint(pixel_key, (SCANS, NBLK * BLK), 0, TILE)
    flagged = jax.random.randint(flag_key, (SCANS, NBLK * BLK), 0, 8) == 0
    return jnp.where(flagged, -1, pixels).astype(jnp.int32)


def steps_of(own_key, extent, cuts, smallest, top_value):
    gain = 1.0
    for axis_at, shards_of in cuts:
        steps = jax.random.uniform(jax.random.fold_in(jax.random.fold_in(own_key, 6), axis_at), (shards_of,), jnp.float32, smallest / len(cuts), top_value / len(cuts))
        gain = gain * jnp.repeat(jnp.exp(steps), extent[axis_at] // shards_of).reshape((-1,) + (1,) * (len(extent) - 1 - axis_at))
    return gain


def gaussian(rng, extent, width, reach, cuts=(), held_as=jnp.bfloat16):
    values = width * jax.random.normal(rng, extent, jnp.float32)
    if cuts:
        values = values * steps_of(rng, extent, cuts, -0.22, 0.18)
    return jnp.clip(values, -reach, reach).astype(held_as)


def setup_inputs(seed: int = 0) -> dict:
    keys = jax.random.split(jax.random.key(seed), 11)
    return {
        "field_mix": gaussian(keys[0], (FIELDS, FIELDS), FIELDS ** -0.5, 1.0, ((0, 2),), jnp.float32),
        "alm": gaussian(keys[1], (ORDERS, 2, FIELDS, ELLS), 1.0, 6.0, ((0, 16), (2, 2))),
        "legendre": gaussian(keys[2], (ORDERS, ELLS, CYCLES), ELLS ** -0.5, 0.125, ((0, 16),)),
        "order_ids": jax.random.permutation(keys[3], ORDERS).astype(jnp.int32),
        "fetch_list": draw_fetch_list(jax.random.fold_in(keys[10], 71), 0),
        "scan_tiles": draw_scan_tiles(jax.random.fold_in(keys[10], 71), 0),
        "block_tile": draw_block_tile(jax.random.fold_in(keys[10], 71), 0),
        "block_pix": draw_block_pix(jax.random.fold_in(keys[10], 71), 0),
        "noise_kernel": gaussian(keys[8], (SCANS, KW), 0.04, 0.24, ((0, 16),), jnp.float32),
        "scan_weight": jnp.clip(jnp.exp(math.log(1.0) - 2.3025851 * jax.random.uniform(keys[9], (SCANS,), jnp.float32) ** steps_of(keys[9], (SCANS,), ((0, 16),), -0.2, 0.2)), 0.1, 1.0),
    }


def reference(field_mix, alm, legendre, order_ids, fetch_list, scan_tiles, block_tile, block_pix, noise_kernel, scan_weight):
    highest = lax.Precision.HIGHEST

    def order_cycles(operands):
        coeffs, table = operands
        mixed_alm = jnp.einsum('fg,cgl->cfl', field_mix, coeffs.astype(jnp.float32), precision=highest).astype(jnp.bfloat16)
        return jnp.einsum('cfl,lr->rcf', mixed_alm.astype(jnp.float32), table.astype(jnp.float32)).astype(jnp.bfloat16)
    cycle_coeff = lax.map(order_cycles, (alm, legendre))
    by_cycle = jnp.transpose(cycle_coeff, (1, 0, 2, 3))
    pixel_iota = jnp.arange(NPHI, dtype=jnp.int32)
    phase_steps = order_ids[:, None] * (2 * pixel_iota[None, :] + 1) % (2 * NPHI)
    angles = phase_steps.astype(jnp.float32) * (math.pi / NPHI)
    weights = jnp.where(order_ids == 0, 1.0, 2.0).astype(jnp.float32) / math.sqrt(2.0 * ORDERS)
    fourier = jnp.stack([weights[:, None] * jnp.cos(angles), -weights[:, None] * jnp.sin(angles)], axis=1).astype(jnp.bfloat16)
    fourier_wide = fourier.astype(jnp.float32)

    def cycle_pixels(coeffs):
        return jnp.einsum('scf,scj->fj', coeffs.astype(jnp.float32), fourier_wide).astype(jnp.bfloat16)
    cycle_maps = lax.map(cycle_pixels, by_cycle)
    flat_map = jnp.transpose(cycle_maps, (1, 0, 2)).reshape(FIELDS, CYCLES * NPHI)
    scan_iota = jnp.arange(SCANS, dtype=jnp.int32)
    holder = scan_iota // SCAN_DEV
    slot_index = jnp.take_along_axis(scan_tiles, block_tile, axis=1)
    source = slot_index // CAP
    within = slot_index % CAP
    local_tile = fetch_list[source, holder[:, None], within]
    global_tile = source * TILES_DEV + local_tile
    pixels = block_pix.reshape(SCANS, NBLK, BLK)
    valid_mask = (pixels >= 0).reshape(SCANS, NBLK * BLK)
    target = (global_tile[:, :, None] * TILE + jnp.maximum(pixels, 0)).reshape(SCANS, NBLK * BLK)
    scan_length = NBLK * BLK
    padded_length = 1 << int(math.ceil(math.log2(scan_length + KW)))
    taps = lax.optimization_barrier(noise_kernel.astype(jnp.bfloat16)).astype(jnp.float32)
    response = jnp.zeros((SCANS, padded_length), jnp.float32)
    response = response.at[:, :KW].set(taps)
    response = response.at[:, padded_length - KW + 1:].set(taps[:, 1:][:, ::-1])

    def scan_step(total, operands):
        spots, mask_row, answer, weight = operands
        samples = jnp.where(mask_row[None, :], flat_map[:, spots], 0).astype(jnp.float32)
        spectrum = jnp.fft.rfft(samples, n=padded_length, axis=-1) * jnp.fft.rfft(answer)[None, :]
        filtered = jnp.fft.irfft(spectrum, n=padded_length, axis=-1)[:, :scan_length]
        weighted = lax.optimization_barrier((weight * filtered).astype(jnp.bfloat16)).astype(jnp.float32)
        destination = jnp.where(mask_row, spots, CYCLES * NPHI)
        total = total.at[:, destination].add(weighted, mode='drop')
        return (total, None)
    initial = jnp.zeros((FIELDS, CYCLES * NPHI), jnp.float32)
    binned_flat, unused = lax.scan(scan_step, initial, (target, valid_mask, response, scan_weight))
    return binned_flat.reshape(FIELDS, CYCLES, NPHI).transpose(1, 0, 2)
```

```python
import functools
import math

import jax
import jax.numpy as jnp
from jax import lax
from jax.experimental import pallas as pl
from jax.experimental.pallas import tpu as pltpu
from jax.sharding import PartitionSpec as P

NPHI = 4096
TILE = 128
COLS = 256
VMEM = pltpu.VMEM
SMEM = pltpu.SMEM


def scan_kernel(
    scan_tiles, block_tile, scan_weight, tiles, pix, noise, out, table, padded
):
    scan_count, block_total = block_tile.shape
    length = pix.shape[1]
    block_len = length // block_total
    lags = noise.shape[1]
    fields = tiles.shape[1]
    per_block = block_len // COLS
    halo = lags // COLS
    window = 2 * lags + COLS
    rows = (length // COLS) * fields
    chunk_blocks = 8
    while block_total % chunk_blocks:
        chunk_blocks //= 2
    chunk_rows = chunk_blocks * per_block * fields

    out[...] = jnp.zeros(out.shape, out.dtype)
    padded[pl.ds(0, halo * fields), :] = jnp.zeros((halo * fields, COLS), padded.dtype)
    padded[pl.ds(halo * fields + rows, halo * fields), :] = jnp.zeros(
        (halo * fields, COLS), padded.dtype
    )
    taps = noise[...].astype(jnp.bfloat16).astype(jnp.float32)
    lane = lax.broadcasted_iota(jnp.int32, taps.shape, 1)
    moved = jnp.where(lane == lags - 1, 0.0, pltpu.roll(taps, lags - 1, 1))
    turn = (
        lax.broadcasted_iota(jnp.int32, (TILE, TILE), 0)
        + lax.broadcasted_iota(jnp.int32, (TILE, TILE), 1)
        == TILE - 1
    ).astype(jnp.float32).astype(jnp.bfloat16)
    chunks = lags // TILE
    blank = jnp.zeros((scan_count, TILE), jnp.float32)
    turned = [
        jnp.dot(
            moved[:, c * TILE : (c + 1) * TILE].astype(jnp.bfloat16),
            turn,
            preferred_element_type=jnp.float32,
        )
        for c in range(chunks)
    ]
    band = jnp.concatenate([blank] + turned[::-1] + [taps] + [blank] * 2, axis=1)
    width = band.shape[1]
    top = width - COLS
    for n in range(scan_count):
        strip = pltpu.roll(
            jnp.broadcast_to(band[n : n + 1], (TILE, width)), 0, 1, stride=1, stride_axis=0
        ).astype(jnp.bfloat16)
        for q in range(window // TILE):
            start = top - q * TILE
            table[n, q * TILE : (q + 1) * TILE, :] = strip[:, start : start + COLS]

    def one_scan(n):
        def sample(b, carry):
            slot = scan_tiles[n, block_tile[n, b]]
            tile = tiles[slot].astype(jnp.float32)
            for c in range(block_len // TILE):
                at = pl.multiple_of(b * block_len + c * TILE, TILE)
                index = jnp.broadcast_to(pix[n : n + 1, pl.ds(at, TILE)], tile.shape)
                value = jnp.take_along_axis(
                    tile, jnp.maximum(index, 0), axis=1, mode="promise_in_bounds"
                )
                value = jnp.where(index >= 0, value, 0.0).astype(padded.dtype)
                row = pl.multiple_of((b * per_block + (c * TILE) // COLS + halo) * fields, 16)
                lane_at = (c * TILE) % COLS
                padded[pl.ds(row, fields), lane_at : lane_at + TILE] = value
            return carry

        lax.fori_loop(0, block_total, sample, 0, unroll=4)
        weight = scan_weight[n]

        def chunk(m, carry):
            base = m * chunk_rows
            pieces = [
                padded[pl.ds(pl.multiple_of(base + o * fields, 16), chunk_rows), :]
                for o in range(2 * halo + 1)
            ]
            filtered = jnp.dot(
                jnp.concatenate(pieces, axis=1), table[n], preferred_element_type=jnp.float32
            )
            weighted = (weight * filtered).astype(jnp.bfloat16)
            for k in range(chunk_blocks):
                b = m * chunk_blocks + k
                at = pl.multiple_of(b * block_len, TILE)
                index = pix[n : n + 1, pl.ds(at, block_len)]
                hot = (
                    lax.broadcasted_iota(jnp.int32, (TILE, block_len), 0) == index
                ).astype(jnp.float32).astype(jnp.bfloat16)
                first = k * per_block * fields
                row = jnp.concatenate(
                    [
                        weighted[first + i * fields : first + (i + 1) * fields]
                        for i in range(per_block)
                    ],
                    axis=1,
                )
                part = lax.dot_general(
                    row, hot, (((1,), (1,)), ((), ())), preferred_element_type=jnp.float32
                )
                slot = scan_tiles[n, block_tile[n, b]]
                out[slot] += part
            return carry

        lax.fori_loop(0, block_total // chunk_blocks, chunk, 0)

    for n in range(scan_count):
        one_scan(n)


def scan_part(tiles, scan_tiles, block_tile, block_pix, noise_kernel, scan_weight):
    scan_count, lags = noise_kernel.shape
    fields = tiles.shape[1]
    length = block_pix.shape[1]
    return pl.pallas_call(
        scan_kernel,
        out_shape=jax.ShapeDtypeStruct(tiles.shape, jnp.float32),
        in_specs=[pl.BlockSpec(memory_space=SMEM)] * 3 + [pl.BlockSpec(memory_space=VMEM)] * 3,
        out_specs=pl.BlockSpec(memory_space=VMEM),
        scratch_shapes=[
            VMEM((scan_count, 2 * lags + COLS, COLS), jnp.bfloat16),
            VMEM(((length + 2 * lags) // COLS * fields, COLS), jnp.bfloat16),
        ],
        compiler_params=pltpu.CompilerParams(vmem_limit_bytes=40 * 2**20),
        name="scans",
    )(scan_tiles, block_tile, scan_weight, tiles, block_pix, noise_kernel)


def local(
    field_mix,
    alm,
    legendre,
    order_ids,
    fetch_list,
    scan_tiles,
    block_tile,
    block_pix,
    noise_kernel,
    scan_weight,
):
    highest = lax.Precision.HIGHEST
    device_count = lax.axis_size("dev")
    position = lax.axis_index("dev")
    halves = lax.axis_size("half")
    own = jnp.einsum(
        "scgl,slr->rscg", alm, legendre, preferred_element_type=jnp.float32
    )
    both = lax.all_gather(own, "half", axis=3, tiled=True)
    mixed = jnp.einsum("fg,rscg->rscf", field_mix, both, precision=highest).astype(jnp.bfloat16)
    by_cycle = lax.all_to_all(mixed, "dev", split_axis=0, concat_axis=1, tiled=True)
    cycle_count, order_count, _, field_count = by_cycle.shape
    weights = jnp.where(order_ids == 0, 1.0, 2.0).astype(jnp.float32) / math.sqrt(2.0 * order_count)
    per_cycle = NPHI // TILE
    pieces = jnp.arange(per_cycle, dtype=jnp.int32)
    inner = jnp.arange(TILE, dtype=jnp.int32)
    outer_angle = (order_ids[:, None] * (2 * TILE * pieces[None, :]) % (2 * NPHI)).astype(
        jnp.float32
    ) * (math.pi / NPHI)
    inner_angle = (order_ids[:, None] * (2 * inner[None, :] + 1) % (2 * NPHI)).astype(
        jnp.float32
    ) * (math.pi / NPHI)
    real = by_cycle[:, :, 0].astype(jnp.float32) * weights[None, :, None]
    imag = by_cycle[:, :, 1].astype(jnp.float32) * weights[None, :, None]
    cos_out = jnp.cos(outer_angle).T[None, :, None, :]
    sin_out = jnp.sin(outer_angle).T[None, :, None, :]
    real = real.transpose(0, 2, 1)[:, None]
    imag = imag.transpose(0, 2, 1)[:, None]
    turned = jnp.concatenate(
        [real * cos_out - imag * sin_out, -(real * sin_out + imag * cos_out)], axis=-1
    )
    basis = jnp.concatenate([jnp.cos(inner_angle), jnp.sin(inner_angle)], axis=0)
    map_tiles = jnp.einsum("rafm,mb->rafb", turned, basis, precision=highest).astype(jnp.bfloat16)
    map_tiles = map_tiles.reshape(cycle_count * per_cycle, field_count, TILE)
    tile_count = map_tiles.shape[0]
    slot_capacity = fetch_list.shape[2]
    owner_row = lax.dynamic_index_in_dim(fetch_list, position, 0, keepdims=False)
    outgoing = map_tiles[jnp.maximum(owner_row, 0)]
    fetched = lax.all_to_all(outgoing, "dev", split_axis=0, concat_axis=0, tiled=True)
    slot_total = device_count * slot_capacity
    flat_fetched = fetched.reshape(slot_total, field_count, TILE)
    per_slot = scan_part(
        flat_fetched, scan_tiles, block_tile, block_pix, noise_kernel, scan_weight
    )
    per_slot = per_slot.reshape(device_count, slot_capacity, field_count, TILE)
    returned = lax.all_to_all(per_slot, "dev", split_axis=0, concat_axis=0, tiled=True)
    owner_select = (
        jnp.arange(tile_count, dtype=jnp.int32)[:, None] == owner_row.reshape(-1)[None, :]
    ).astype(jnp.float32)
    own_tiles = jnp.dot(
        owner_select, returned.reshape(slot_total, field_count * TILE), precision=highest
    )
    binned = own_tiles.reshape(cycle_count, NPHI // TILE, field_count, TILE).transpose(0, 2, 1, 3)
    return binned.reshape(cycle_count, field_count, NPHI)


def solution(mesh):
    return jax.shard_map(
        local,
        mesh=mesh,
        in_specs=(
            P("half", None),
            P("dev", None, "half", None),
            P("dev", None, None),
            P(),
            P(),
            P("dev", None),
            P("dev", None),
            P("dev", None),
            P("dev", None),
            P("dev"),
        ),
        out_specs=P("dev", "half", None),
        check_vma=False,
    )
```

```python
import functools
import math

import jax
import jax.numpy as jnp
from jax import lax
from jax.experimental import pallas as pl
from jax.experimental.pallas import tpu as pltpu
from jax.sharding import PartitionSpec as P

NPHI = 4096
TILE = 128
COLS = 256
VMEM = pltpu.VMEM
SMEM = pltpu.SMEM


def scan_kernel(
    scan_tiles, block_tile, scan_weight, tiles, pix, noise, out, table, padded, sums
):
    scan_count, block_total = block_tile.shape
    length = pix.shape[1]
    block_len = length // block_total
    lags = noise.shape[1]
    fields = tiles.shape[1]
    per_block = block_len // COLS
    halo = lags // COLS
    window = 2 * lags + COLS
    rows = (length // COLS) * fields
    chunk_blocks = 8
    while block_total % chunk_blocks:
        chunk_blocks //= 2
    chunk_rows = chunk_blocks * per_block * fields

    sums[...] = jnp.zeros(sums.shape, sums.dtype)
    padded[pl.ds(0, halo * fields), :] = jnp.zeros((halo * fields, COLS), padded.dtype)
    padded[pl.ds(halo * fields + rows, halo * fields), :] = jnp.zeros(
        (halo * fields, COLS), padded.dtype
    )
    taps = noise[...].astype(jnp.bfloat16).astype(jnp.float32)
    lane = lax.broadcasted_iota(jnp.int32, taps.shape, 1)
    moved = jnp.where(lane == lags - 1, 0.0, pltpu.roll(taps, lags - 1, 1))
    turn = (
        lax.broadcasted_iota(jnp.int32, (TILE, TILE), 0)
        + lax.broadcasted_iota(jnp.int32, (TILE, TILE), 1)
        == TILE - 1
    ).astype(jnp.float32).astype(jnp.bfloat16)
    chunks = lags // TILE
    blank = jnp.zeros((scan_count, TILE), jnp.float32)
    turned = [
        jnp.dot(
            moved[:, c * TILE : (c + 1) * TILE].astype(jnp.bfloat16),
            turn,
            preferred_element_type=jnp.float32,
        )
        for c in range(chunks)
    ]
    band = jnp.concatenate([blank] + turned[::-1] + [taps] + [blank] * 2, axis=1)
    width = band.shape[1]
    top = width - COLS
    for n in range(scan_count):
        strip = pltpu.roll(
            jnp.broadcast_to(band[n : n + 1], (TILE, width)), 0, 1, stride=1, stride_axis=0
        ).astype(jnp.bfloat16)
        for q in range(window // TILE):
            start = top - q * TILE
            table[n, q * TILE : (q + 1) * TILE, :] = strip[:, start : start + COLS]

    def one_scan(n):
        def sample(b, carry):
            slot = scan_tiles[n, block_tile[n, b]]
            tile = tiles[slot].astype(jnp.float32)
            for c in range(block_len // TILE):
                at = pl.multiple_of(b * block_len + c * TILE, TILE)
                index = jnp.broadcast_to(pix[n : n + 1, pl.ds(at, TILE)], tile.shape)
                value = jnp.take_along_axis(
                    tile, jnp.maximum(index, 0), axis=1, mode="promise_in_bounds"
                )
                value = jnp.where(index >= 0, value, 0.0).astype(padded.dtype)
                row = pl.multiple_of((b * per_block + (c * TILE) // COLS + halo) * fields, 16)
                lane_at = (c * TILE) % COLS
                padded[pl.ds(row, fields), lane_at : lane_at + TILE] = value
            return carry

        lax.fori_loop(0, block_total, sample, 0, unroll=4)
        weight = scan_weight[n]

        def chunk(m, carry):
            base = m * chunk_rows
            pieces = [
                padded[pl.ds(pl.multiple_of(base + o * fields, 16), chunk_rows), :]
                for o in range(2 * halo + 1)
            ]
            filtered = jnp.dot(
                jnp.concatenate(pieces, axis=1), table[n], preferred_element_type=jnp.float32
            )
            weighted = (weight * filtered).astype(jnp.bfloat16)
            for k in range(chunk_blocks):
                b = m * chunk_blocks + k
                at = pl.multiple_of(b * block_len, TILE)
                index = pix[n : n + 1, pl.ds(at, block_len)]
                hot = (
                    lax.broadcasted_iota(jnp.int32, (TILE, block_len), 0) == index
                ).astype(jnp.float32).astype(jnp.bfloat16)
                first = k * per_block * fields
                row = jnp.concatenate(
                    [
                        weighted[first + i * fields : first + (i + 1) * fields]
                        for i in range(per_block)
                    ],
                    axis=1,
                )
                part = lax.dot_general(
                    row, hot, (((1,), (1,)), ((), ())), preferred_element_type=jnp.float32
                )
                slot = scan_tiles[n, block_tile[n, b]]
                sums[slot] += part
            return carry

        lax.fori_loop(0, block_total // chunk_blocks, chunk, 0)

    for n in range(scan_count):
        one_scan(n)
    out[...] = sums[...].astype(out.dtype)


def scan_part(tiles, scan_tiles, block_tile, block_pix, noise_kernel, scan_weight):
    scan_count, lags = noise_kernel.shape
    fields = tiles.shape[1]
    length = block_pix.shape[1]
    return pl.pallas_call(
        scan_kernel,
        out_shape=jax.ShapeDtypeStruct(tiles.shape, jnp.bfloat16),
        in_specs=[pl.BlockSpec(memory_space=SMEM)] * 3 + [pl.BlockSpec(memory_space=VMEM)] * 3,
        out_specs=pl.BlockSpec(memory_space=VMEM),
        scratch_shapes=[
            VMEM((scan_count, 2 * lags + COLS, COLS), jnp.bfloat16),
            VMEM(((length + 2 * lags) // COLS * fields, COLS), jnp.bfloat16),
            VMEM(tiles.shape, jnp.float32),
        ],
        compiler_params=pltpu.CompilerParams(vmem_limit_bytes=40 * 2**20),
        name="scans",
    )(scan_tiles, block_tile, scan_weight, tiles, block_pix, noise_kernel)


MESH = pl.DeviceIdType.MESH
HIGHEST = lax.Precision.HIGHEST
SIDES = (((1,), (1,)), ((), ()))


def cos_sin(steps):
    quarter = NPHI // 2
    turn = (steps + quarter // 2) // quarter
    x = (steps - turn * quarter).astype(jnp.float32) * (math.pi / NPHI)
    y = x * x
    sin = x * (1 + y * (-1 / 6 + y * (1 / 120 + y * (-1 / 5040 + y / 362880))))
    cos = 1 + y * (-1 / 2 + y * (1 / 24 + y * (-1 / 720 + y * (1 / 40320 - y / 3628800))))
    odd = turn % 2 == 1
    cos_sign = jnp.where((turn == 1) | (turn == 2), -1.0, 1.0)
    sin_sign = jnp.where((turn == 2) | (turn == 3), -1.0, 1.0)
    return jnp.where(odd, sin, cos) * cos_sign, jnp.where(odd, cos, sin) * sin_sign


def meet(count, peer):
    barrier = pltpu.get_barrier_semaphore()

    def greet(i, carry):
        pl.semaphore_signal(barrier, inc=1, device_id=peer(i), device_id_type=MESH)
        return carry

    lax.fori_loop(1, count, greet, 0)
    return lambda: pl.semaphore_wait(barrier, count - 1)


def map_kernel(
    owner, orders, mix, alm, legendre, out, coeff_out, coeff_in, tiles, tiles_out, tiles_in,
    sent, got, tile_sent, tile_got,
):
    half, dev = lax.axis_index("half"), lax.axis_index("dev")
    halves, devs = lax.axis_size("half"), lax.axis_size("dev")
    everyone = halves * devs
    mine = half * devs + dev
    fields = mix.shape[0]
    caps = owner.shape[0]
    cycles = coeff_out.shape[0]
    groups = coeff_out.shape[1]
    slots = alm.shape[0] // (2 * fields)

    def any_peer(i):
        other = lax.rem(mine + i, everyone)
        return {"half": other // devs, "dev": lax.rem(other, devs)}

    ready = meet(everyone, any_peer)
    full = lax.dot_general(legendre[...], alm[...], SIDES, preferred_element_type=jnp.float32)
    lane = lax.broadcasted_iota(jnp.int32, (cycles, full.shape[1]), 1) // (2 * fields)
    own = jnp.zeros((cycles, full.shape[1]), jnp.float32)
    for s in range(slots):
        own = jnp.where(lane == s, full[s * cycles : (s + 1) * cycles], own)
    for q in range(groups):
        coeff_out[:, q, :] = own[:, q * TILE : (q + 1) * TILE]
    ready()

    def coeff_copy(target_half, target_dev, from_half, from_dev, n_out, n_in):
        return pltpu.make_async_remote_copy(
            src_ref=coeff_out.at[target_dev],
            dst_ref=coeff_in.at[from_half, from_dev],
            send_sem=sent.at[n_out],
            recv_sem=got.at[n_in],
            device_id={"half": target_half, "dev": target_dev},
            device_id_type=MESH,
        )

    def send_coeff(i, carry):
        other = lax.rem(mine + i, everyone)
        coeff_copy(other // devs, lax.rem(other, devs), half, dev, other, mine).start()
        return carry

    lax.fori_loop(1, everyone, send_coeff, 0)
    coeff_in[half, dev] = coeff_out[dev]

    ids = orders[...]
    total = ids.shape[1]
    per_cycle = NPHI // TILE
    weight = jnp.where(ids == 0, 1.0, 2.0) / math.sqrt(2.0 * total)
    outer = lax.broadcasted_iota(jnp.int32, (per_cycle, total), 0) * (2 * TILE)
    inner = lax.broadcasted_iota(jnp.int32, (TILE, total), 0) * 2 + 1
    cos_out, sin_out = cos_sin(outer * ids % (2 * NPHI))
    basis = jnp.concatenate(cos_sin(inner * ids % (2 * NPHI)), axis=1)
    spread = []
    row_field = lax.broadcasted_iota(jnp.int32, (2 * fields, fields), 0) % fields
    pick_row = row_field == lax.broadcasted_iota(jnp.int32, (2 * fields, fields), 1)
    wide = (2 * fields, TILE)
    same = lax.broadcasted_iota(jnp.int32, wide, 0) // fields == (
        lax.broadcasted_iota(jnp.int32, wide, 1) // fields
    ) % 2
    for h in range(halves):
        lanes = (mix.shape[1], TILE)
        pick_lane = lax.broadcasted_iota(jnp.int32, lanes, 0) == (
            lax.broadcasted_iota(jnp.int32, lanes, 1) % fields + h * fields
        )
        rows = jnp.dot(
            pick_row.astype(jnp.float32), mix[...], precision=HIGHEST,
            preferred_element_type=jnp.float32,
        )
        rows = jnp.dot(
            rows, pick_lane.astype(jnp.float32), precision=HIGHEST,
            preferred_element_type=jnp.float32,
        )
        spread.append(jnp.where(same, rows, 0.0))

    def wait_coeff(i, carry):
        other = lax.rem(mine + i, everyone)
        copy = coeff_copy(
            other // devs, lax.rem(other, devs), other // devs, lax.rem(other, devs), other, other
        )
        copy.wait_recv()
        copy.wait_send()
        return carry

    lax.fori_loop(1, everyone, wait_coeff, 0)
    coeff = jnp.zeros((2 * fields, total), jnp.float32)
    per_group = slots // groups
    for h in range(halves):
        block = jnp.concatenate([coeff_in[h, :, q, :] for q in range(groups)], axis=0)
        group = lax.broadcasted_iota(jnp.int32, block.shape, 1) // (2 * fields)
        block = jnp.concatenate(
            [jnp.where(group == s, block, 0.0) for s in range(per_group)], axis=0
        )
        coeff = coeff + lax.dot_general(
            spread[h], block, SIDES, precision=HIGHEST, preferred_element_type=jnp.float32
        )
    coeff = coeff * weight
    real, imag = coeff[:fields], coeff[fields:]
    turned = []
    for a in range(per_cycle):
        c, s = cos_out[a : a + 1], sin_out[a : a + 1]
        turned.append(jnp.concatenate([real * c - imag * s, -(real * s + imag * c)], axis=1))
    pixels = lax.dot_general(
        jnp.concatenate(turned, axis=0), basis, SIDES, precision=HIGHEST,
        preferred_element_type=jnp.float32,
    ).astype(jnp.bfloat16)
    for a in range(per_cycle):
        tiles[a] = pixels[a * fields : (a + 1) * fields]

    def tile_copy(target, source):
        return pltpu.make_async_remote_copy(
            src_ref=tiles_out.at[target],
            dst_ref=tiles_in.at[source],
            send_sem=tile_sent.at[target],
            recv_sem=tile_got.at[source],
            device_id={"half": half, "dev": target},
            device_id_type=MESH,
        )

    def send_tiles(i, carry):
        other = lax.rem(dev + i, devs)
        for k in range(caps):
            tiles_out[other, k] = tiles[jnp.maximum(owner[k, other], 0)]
        tile_copy(other, dev).start()
        return carry

    lax.fori_loop(1, devs, send_tiles, 0)
    for k in range(caps):
        tiles_in[dev, k] = tiles[jnp.maximum(owner[k, dev], 0)]

    def wait_tiles(i, carry):
        other = lax.rem(dev + i, devs)
        pltpu.make_async_remote_copy(
            src_ref=tiles_out.at[other],
            dst_ref=tiles_in.at[other],
            send_sem=tile_sent.at[other],
            recv_sem=tile_got.at[other],
            device_id={"half": half, "dev": other},
            device_id_type=MESH,
        ).wait()
        return carry

    lax.fori_loop(1, devs, wait_tiles, 0)
    out[...] = tiles_in[...]


def map_part(owner, orders, field_mix, alm, legendre, devs, halves):
    caps = owner.shape[0]
    fields = field_mix.shape[0]
    groups = alm.shape[0] // TILE
    cycles = legendre.shape[0] * 2 * fields // alm.shape[0]
    return pl.pallas_call(
        map_kernel,
        out_shape=jax.ShapeDtypeStruct((devs, caps, fields, TILE), jnp.bfloat16),
        in_specs=[pl.BlockSpec(memory_space=SMEM)] + [pl.BlockSpec(memory_space=VMEM)] * 4,
        out_specs=pl.BlockSpec(memory_space=VMEM),
        scratch_shapes=[
            VMEM((cycles, groups, TILE), jnp.float32),
            VMEM((halves, devs, groups, TILE), jnp.float32),
            VMEM((NPHI // TILE, fields, TILE), jnp.bfloat16),
            VMEM((devs, caps, fields, TILE), jnp.bfloat16),
            VMEM((devs, caps, fields, TILE), jnp.bfloat16),
            pltpu.SemaphoreType.DMA((halves * devs,)),
            pltpu.SemaphoreType.DMA((halves * devs,)),
            pltpu.SemaphoreType.DMA((devs,)),
            pltpu.SemaphoreType.DMA((devs,)),
        ],
        compiler_params=pltpu.CompilerParams(
            collective_id=0, has_side_effects=True, vmem_limit_bytes=48 * 2**20
        ),
        name="maps",
    )(owner, orders, field_mix, alm, legendre)


def return_kernel(parts, out, held, sent, got):
    half, dev = lax.axis_index("half"), lax.axis_index("dev")
    devs = lax.axis_size("dev")

    def peer(i):
        return {"half": half, "dev": lax.rem(dev + i, devs)}

    meet(devs, peer)()

    def copy(target, source):
        return pltpu.make_async_remote_copy(
            src_ref=parts.at[target],
            dst_ref=held.at[source],
            send_sem=sent.at[target],
            recv_sem=got.at[source],
            device_id={"half": half, "dev": target},
            device_id_type=MESH,
        )

    def send(i, carry):
        copy(lax.rem(dev + i, devs), dev).start()
        return carry

    lax.fori_loop(1, devs, send, 0)
    held[dev] = parts[dev]

    def wait(i, carry):
        other = lax.rem(dev + i, devs)
        copy(other, other).wait()
        return carry

    lax.fori_loop(1, devs, wait, 0)
    out[...] = held[...]


def return_part(parts, devs):
    return pl.pallas_call(
        return_kernel,
        out_shape=jax.ShapeDtypeStruct(parts.shape, parts.dtype),
        in_specs=[pl.BlockSpec(memory_space=VMEM)],
        out_specs=pl.BlockSpec(memory_space=VMEM),
        scratch_shapes=[
            VMEM(parts.shape, parts.dtype),
            pltpu.SemaphoreType.DMA((devs,)),
            pltpu.SemaphoreType.DMA((devs,)),
        ],
        compiler_params=pltpu.CompilerParams(
            collective_id=1, has_side_effects=True, vmem_limit_bytes=32 * 2**20
        ),
        name="returns",
    )(parts)


def place_kernel(owner, parts, out):
    caps = owner.shape[0]
    out[...] = jnp.zeros(out.shape, out.dtype)

    def one(e, carry):
        for k in range(caps):
            tile = owner[k, e]
            at = pl.ds(pl.multiple_of(jnp.maximum(tile, 0) * TILE, TILE), TILE)
            out[0, :, at] += jnp.where(tile >= 0, parts[e, k].astype(out.dtype), 0.0)
        return carry

    lax.fori_loop(0, owner.shape[1], one, 0)


def place_part(owner, parts):
    return pl.pallas_call(
        place_kernel,
        out_shape=jax.ShapeDtypeStruct((1, parts.shape[2], NPHI), jnp.float32),
        in_specs=[pl.BlockSpec(memory_space=SMEM), pl.BlockSpec(memory_space=VMEM)],
        out_specs=pl.BlockSpec(memory_space=VMEM),
        compiler_params=pltpu.CompilerParams(vmem_limit_bytes=32 * 2**20),
        name="placing",
    )(owner, parts)


def local(
    field_mix,
    alm,
    legendre,
    order_ids,
    fetch_list,
    scan_tiles,
    block_tile,
    block_pix,
    noise_kernel,
    scan_weight,
):
    devs = lax.axis_size("dev")
    halves = lax.axis_size("half")
    order_slots, parts, fields, ells = alm.shape
    cycles = legendre.shape[2]
    owner = lax.dynamic_index_in_dim(
        fetch_list.transpose(0, 2, 1), lax.axis_index("dev"), 0, keepdims=False
    )
    per_row = TILE // (parts * fields)
    orders = order_ids.reshape(devs, order_slots // per_row, per_row).transpose(2, 1, 0)
    tiles = map_part(
        owner,
        orders.reshape(1, -1),
        field_mix,
        alm.reshape(order_slots * parts * fields, ells),
        legendre.transpose(0, 2, 1).reshape(order_slots * cycles, ells),
        devs,
        halves,
    )
    per_slot = scan_part(
        tiles.reshape((-1,) + tiles.shape[2:]),
        scan_tiles,
        block_tile,
        block_pix,
        noise_kernel,
        scan_weight,
    )
    returned = return_part(per_slot.reshape(tiles.shape), devs)
    return place_part(owner, returned)


def solution(mesh):
    return jax.shard_map(
        local,
        mesh=mesh,
        in_specs=(
            P("half", None),
            P("dev", None, "half", None),
            P("dev", None, None),
            P(),
            P(),
            P("dev", None),
            P("dev", None),
            P("dev", None),
            P("dev", None),
            P("dev"),
        ),
        out_specs=P("dev", "half", None),
        check_vma=False,
    )
```

```python
import functools
import math

import jax
import jax.numpy as jnp
from jax import lax
from jax.experimental import pallas as pl
from jax.experimental.pallas import tpu as pltpu
from jax.sharding import PartitionSpec as P

NPHI = 4096
TILE = 128
COLS = 256
VMEM = pltpu.VMEM
SMEM = pltpu.SMEM


def scan_kernel(
    scan_tiles, block_tile, scan_weight, tiles, pix, noise, out, table, even, odd, weighted, sums
):
    scan_count, block_total = block_tile.shape
    length = pix.shape[1]
    block_len = length // block_total
    lags = noise.shape[1]
    fields = tiles.shape[1]
    per_block = block_len // COLS
    halo = lags // COLS
    window = 2 * lags + COLS
    rows = (length // COLS) * fields
    sums[...] = jnp.zeros(sums.shape, sums.dtype)
    padded = (even, odd)
    edge = jnp.zeros((halo * fields, COLS), jnp.bfloat16)
    for ref in padded:
        ref[: halo * fields, :] = edge
        ref[halo * fields + rows :, :] = edge
    taps = noise[...].astype(jnp.bfloat16).astype(jnp.float32)
    lane = lax.broadcasted_iota(jnp.int32, taps.shape, 1)
    moved = jnp.where(lane == lags - 1, 0.0, pltpu.roll(taps, lags - 1, 1))
    turn = (
        lax.broadcasted_iota(jnp.int32, (TILE, TILE), 0)
        + lax.broadcasted_iota(jnp.int32, (TILE, TILE), 1)
        == TILE - 1
    ).astype(jnp.float32).astype(jnp.bfloat16)
    chunks = lags // TILE
    blank = jnp.zeros((scan_count, TILE), jnp.float32)
    turned = [
        jnp.dot(
            moved[:, c * TILE : (c + 1) * TILE].astype(jnp.bfloat16),
            turn,
            preferred_element_type=jnp.float32,
        )
        for c in range(chunks)
    ]
    band = jnp.concatenate([blank] + turned[::-1] + [taps] + [blank] * 2, axis=1)
    width = band.shape[1]
    top = width - COLS
    for n in range(scan_count):
        strip = pltpu.roll(
            jnp.broadcast_to(band[n : n + 1], (TILE, width)), 0, 1, stride=1, stride_axis=0
        ).astype(jnp.bfloat16)
        for q in range(window // TILE):
            start = top - q * TILE
            table[n, q * TILE : (q + 1) * TILE, :] = strip[:, start : start + COLS]

    below = lax.broadcasted_iota(jnp.int32, (TILE, block_len), 0).astype(jnp.float32).astype(
        jnp.bfloat16
    )

    def sample(n, b):
        slot = scan_tiles[n, block_tile[n, b]]
        tile = tiles[slot].astype(jnp.float32)
        for c in range(block_len // TILE):
            at = pl.multiple_of(b * block_len + c * TILE, TILE)
            index = jnp.broadcast_to(pix[n : n + 1, pl.ds(at, TILE)], tile.shape)
            value = jnp.take_along_axis(
                tile, jnp.maximum(index, 0), axis=1, mode="promise_in_bounds"
            )
            value = jnp.where(index >= 0, value, 0.0).astype(jnp.bfloat16)
            row = pl.multiple_of((b * per_block + (c * TILE) // COLS + halo) * fields, 16)
            lane_at = (c * TILE) % COLS
            padded[n % 2][pl.ds(row, fields), lane_at : lane_at + TILE] = value

    def collect(n, b):
        at = pl.multiple_of(b * block_len, TILE)
        index = pix[n : n + 1, pl.ds(at, block_len)].astype(jnp.float32).astype(jnp.bfloat16)
        hot = jnp.where(
            below == index, jnp.ones((), jnp.bfloat16), jnp.zeros((), jnp.bfloat16)
        )
        row = jnp.concatenate(
            [
                weighted[pl.ds(pl.multiple_of((b * per_block + i) * fields, 16), fields), :]
                for i in range(per_block)
            ],
            axis=1,
        )
        part = lax.dot_general(
            row, hot, (((1,), (1,)), ((), ())), preferred_element_type=jnp.float32
        )
        slot = scan_tiles[n, block_tile[n, b]]
        sums[slot] += part

    def together(step, group):
        def body(m, carry):
            for k in range(group):
                step(m * group + k)
            return carry

        lax.fori_loop(0, block_total // group, body, 0)

    group = 4
    while block_total % group:
        group //= 2
    together(lambda b: sample(0, b), group)
    for n in range(scan_count):
        pieces = [
            padded[n % 2][o * fields : o * fields + rows, :] for o in range(2 * halo + 1)
        ]
        filtered = jnp.dot(
            jnp.concatenate(pieces, axis=1), table[n], preferred_element_type=jnp.float32
        )
        weighted[...] = (scan_weight[n] * filtered).astype(jnp.bfloat16)

        def step(b):
            collect(n, b)
            if n + 1 < scan_count:
                sample(n + 1, b)

        together(step, group)
    out[...] = sums[...].astype(out.dtype)


def scan_part(tiles, scan_tiles, block_tile, block_pix, noise_kernel, scan_weight):
    scan_count, lags = noise_kernel.shape
    fields = tiles.shape[1]
    length = block_pix.shape[1]
    return pl.pallas_call(
        scan_kernel,
        out_shape=jax.ShapeDtypeStruct(tiles.shape, jnp.bfloat16),
        in_specs=[pl.BlockSpec(memory_space=SMEM)] * 3 + [pl.BlockSpec(memory_space=VMEM)] * 3,
        out_specs=pl.BlockSpec(memory_space=VMEM),
        scratch_shapes=[
            VMEM((scan_count, 2 * lags + COLS, COLS), jnp.bfloat16),
            VMEM(((length + 2 * lags) // COLS * fields, COLS), jnp.bfloat16),
            VMEM(((length + 2 * lags) // COLS * fields, COLS), jnp.bfloat16),
            VMEM((length // COLS * fields, COLS), jnp.bfloat16),
            VMEM(tiles.shape, jnp.float32),
        ],
        compiler_params=pltpu.CompilerParams(vmem_limit_bytes=40 * 2**20),
        name="scans",
    )(scan_tiles, block_tile, scan_weight, tiles, block_pix, noise_kernel)


MESH = pl.DeviceIdType.MESH
HIGHEST = lax.Precision.HIGHEST
SIDES = (((1,), (1,)), ((), ()))


def cos_sin(steps):
    quarter = NPHI // 2
    turn = (steps + quarter // 2) // quarter
    x = (steps - turn * quarter).astype(jnp.float32) * (math.pi / NPHI)
    y = x * x
    sin = x * (1 + y * (-1 / 6 + y * (1 / 120 + y * (-1 / 5040 + y / 362880))))
    cos = 1 + y * (-1 / 2 + y * (1 / 24 + y * (-1 / 720 + y * (1 / 40320 - y / 3628800))))
    odd = turn % 2 == 1
    cos_sign = jnp.where((turn == 1) | (turn == 2), -1.0, 1.0)
    sin_sign = jnp.where((turn == 2) | (turn == 3), -1.0, 1.0)
    return jnp.where(odd, sin, cos) * cos_sign, jnp.where(odd, cos, sin) * sin_sign


def meet(count, peer):
    barrier = pltpu.get_barrier_semaphore()

    def greet(i, carry):
        pl.semaphore_signal(barrier, inc=1, device_id=peer(i), device_id_type=MESH)
        return carry

    lax.fori_loop(1, count, greet, 0)
    return lambda: pl.semaphore_wait(barrier, count - 1)


def map_kernel(
    owner, orders, mix, alm_hbm, legendre_hbm, out, alm, legendre, coeff_out, coeff_in, tiles,
    tiles_out, tiles_in, loaded, sent, got, tile_sent, tile_got,
):
    half, dev = lax.axis_index("half"), lax.axis_index("dev")
    halves, devs = lax.axis_size("half"), lax.axis_size("dev")
    everyone = halves * devs
    mine = half * devs + dev
    fields = mix.shape[0]
    caps = owner.shape[1]
    loads = [
        pltpu.make_async_copy(alm_hbm, alm, loaded.at[0]),
        pltpu.make_async_copy(legendre_hbm, legendre, loaded.at[1]),
    ]
    for load in loads:
        load.start()
    cycles = coeff_out.shape[0]
    groups = coeff_out.shape[1]
    slots = alm.shape[0] // (2 * fields)

    def any_peer(i):
        other = lax.rem(mine + i, everyone)
        return {"half": other // devs, "dev": lax.rem(other, devs)}

    ready = meet(everyone, any_peer)
    for load in loads:
        load.wait()
    full = lax.dot_general(legendre[...], alm[...], SIDES, preferred_element_type=jnp.float32)
    lane = lax.broadcasted_iota(jnp.int32, (cycles, full.shape[1]), 1) // (2 * fields)
    own = jnp.zeros((cycles, full.shape[1]), jnp.float32)
    for s in range(slots):
        own = jnp.where(lane == s, full[s * cycles : (s + 1) * cycles], own)
    for q in range(groups):
        coeff_out[:, q, :] = own[:, q * TILE : (q + 1) * TILE]
    ready()

    def coeff_copy(target_half, target_dev, from_half, from_dev, n_out, n_in):
        return pltpu.make_async_remote_copy(
            src_ref=coeff_out.at[target_dev],
            dst_ref=coeff_in.at[from_half, from_dev],
            send_sem=sent.at[n_out],
            recv_sem=got.at[n_in],
            device_id={"half": target_half, "dev": target_dev},
            device_id_type=MESH,
        )

    def send_coeff(i, carry):
        other = lax.rem(mine + i, everyone)
        coeff_copy(other // devs, lax.rem(other, devs), half, dev, other, mine).start()
        return carry

    lax.fori_loop(1, everyone, send_coeff, 0)
    coeff_in[half, dev] = coeff_out[dev]

    total = orders.shape[1]
    per_group = slots // groups
    place = lax.broadcasted_iota(jnp.int32, (total, total), 1)
    place = place % devs * slots + place // devs % groups * per_group + place // (devs * groups)
    moves = (lax.broadcasted_iota(jnp.int32, (total, total), 0) == place).astype(jnp.float32)
    ids = jnp.dot(
        orders[...].astype(jnp.float32), moves, precision=HIGHEST,
        preferred_element_type=jnp.float32,
    )
    ids = jnp.round(ids).astype(jnp.int32)
    per_cycle = NPHI // TILE
    weight = jnp.where(ids == 0, 1.0, 2.0) / math.sqrt(2.0 * total)
    outer = lax.broadcasted_iota(jnp.int32, (per_cycle, total), 0) * (2 * TILE)
    inner = lax.broadcasted_iota(jnp.int32, (TILE, total), 0) * 2 + 1
    cos_out, sin_out = cos_sin(outer * ids % (2 * NPHI))
    basis = jnp.concatenate(cos_sin(inner * ids % (2 * NPHI)), axis=1)
    spread = []
    row_field = lax.broadcasted_iota(jnp.int32, (2 * fields, fields), 0) % fields
    pick_row = row_field == lax.broadcasted_iota(jnp.int32, (2 * fields, fields), 1)
    wide = (2 * fields, TILE)
    same = lax.broadcasted_iota(jnp.int32, wide, 0) // fields == (
        lax.broadcasted_iota(jnp.int32, wide, 1) // fields
    ) % 2
    for h in range(halves):
        lanes = (mix.shape[1], TILE)
        pick_lane = lax.broadcasted_iota(jnp.int32, lanes, 0) == (
            lax.broadcasted_iota(jnp.int32, lanes, 1) % fields + h * fields
        )
        rows = jnp.dot(
            pick_row.astype(jnp.float32), mix[...], precision=HIGHEST,
            preferred_element_type=jnp.float32,
        )
        rows = jnp.dot(
            rows, pick_lane.astype(jnp.float32), precision=HIGHEST,
            preferred_element_type=jnp.float32,
        )
        spread.append(jnp.where(same, rows, 0.0))

    def wait_coeff(i, carry):
        other = lax.rem(mine + i, everyone)
        copy = coeff_copy(
            other // devs, lax.rem(other, devs), other // devs, lax.rem(other, devs), other, other
        )
        copy.wait_recv()
        copy.wait_send()
        return carry

    lax.fori_loop(1, everyone, wait_coeff, 0)
    coeff = jnp.zeros((2 * fields, total), jnp.float32)
    for h in range(halves):
        block = jnp.concatenate([coeff_in[h, :, q, :] for q in range(groups)], axis=0)
        group = lax.broadcasted_iota(jnp.int32, block.shape, 1) // (2 * fields)
        block = jnp.concatenate(
            [jnp.where(group == s, block, 0.0) for s in range(per_group)], axis=0
        )
        coeff = coeff + lax.dot_general(
            spread[h], block, SIDES, precision=HIGHEST, preferred_element_type=jnp.float32
        )
    coeff = coeff * weight
    real, imag = coeff[:fields], coeff[fields:]
    turned = []
    for a in range(per_cycle):
        c, s = cos_out[a : a + 1], sin_out[a : a + 1]
        turned.append(jnp.concatenate([real * c - imag * s, -(real * s + imag * c)], axis=1))
    pixels = lax.dot_general(
        jnp.concatenate(turned, axis=0), basis, SIDES, precision=HIGHEST,
        preferred_element_type=jnp.float32,
    ).astype(jnp.bfloat16)
    for a in range(per_cycle):
        tiles[a] = pixels[a * fields : (a + 1) * fields]

    def tile_copy(target, source):
        return pltpu.make_async_remote_copy(
            src_ref=tiles_out.at[target],
            dst_ref=tiles_in.at[source],
            send_sem=tile_sent.at[target],
            recv_sem=tile_got.at[source],
            device_id={"half": half, "dev": target},
            device_id_type=MESH,
        )

    def send_tiles(i, carry):
        other = lax.rem(dev + i, devs)
        for k in range(caps):
            tiles_out[other, k] = tiles[jnp.maximum(owner[dev, k, other], 0)]
        tile_copy(other, dev).start()
        return carry

    lax.fori_loop(1, devs, send_tiles, 0)
    for k in range(caps):
        tiles_in[dev, k] = tiles[jnp.maximum(owner[dev, k, dev], 0)]

    def wait_tiles(i, carry):
        other = lax.rem(dev + i, devs)
        pltpu.make_async_remote_copy(
            src_ref=tiles_out.at[other],
            dst_ref=tiles_in.at[other],
            send_sem=tile_sent.at[other],
            recv_sem=tile_got.at[other],
            device_id={"half": half, "dev": other},
            device_id_type=MESH,
        ).wait()
        return carry

    lax.fori_loop(1, devs, wait_tiles, 0)
    out[...] = tiles_in[...]


def map_part(owner, orders, field_mix, alm, legendre, devs, halves):
    caps = owner.shape[1]
    fields = field_mix.shape[0]
    groups = alm.shape[0] // TILE
    cycles = legendre.shape[0] * 2 * fields // alm.shape[0]
    return pl.pallas_call(
        map_kernel,
        out_shape=jax.ShapeDtypeStruct((devs, caps, fields, TILE), jnp.bfloat16),
        in_specs=[pl.BlockSpec(memory_space=SMEM)]
        + [pl.BlockSpec(memory_space=VMEM)] * 2
        + [pl.BlockSpec(memory_space=pltpu.HBM)] * 2,
        out_specs=pl.BlockSpec(memory_space=VMEM),
        scratch_shapes=[
            VMEM(alm.shape, alm.dtype),
            VMEM(legendre.shape, legendre.dtype),
            VMEM((cycles, groups, TILE), jnp.float32),
            VMEM((halves, devs, groups, TILE), jnp.float32),
            VMEM((NPHI // TILE, fields, TILE), jnp.bfloat16),
            VMEM((devs, caps, fields, TILE), jnp.bfloat16),
            VMEM((devs, caps, fields, TILE), jnp.bfloat16),
            pltpu.SemaphoreType.DMA((2,)),
            pltpu.SemaphoreType.DMA((halves * devs,)),
            pltpu.SemaphoreType.DMA((halves * devs,)),
            pltpu.SemaphoreType.DMA((devs,)),
            pltpu.SemaphoreType.DMA((devs,)),
        ],
        compiler_params=pltpu.CompilerParams(
            collective_id=0, has_side_effects=True, vmem_limit_bytes=48 * 2**20
        ),
        name="maps",
    )(owner, orders, field_mix, alm, legendre)


def return_kernel(parts, out, held, sent, got):
    half, dev = lax.axis_index("half"), lax.axis_index("dev")
    devs = lax.axis_size("dev")

    def peer(i):
        return {"half": half, "dev": lax.rem(dev + i, devs)}

    meet(devs, peer)()

    def copy(target, source):
        return pltpu.make_async_remote_copy(
            src_ref=parts.at[target],
            dst_ref=held.at[source],
            send_sem=sent.at[target],
            recv_sem=got.at[source],
            device_id={"half": half, "dev": target},
            device_id_type=MESH,
        )

    def send(i, carry):
        copy(lax.rem(dev + i, devs), dev).start()
        return carry

    lax.fori_loop(1, devs, send, 0)
    held[dev] = parts[dev]

    def wait(i, carry):
        other = lax.rem(dev + i, devs)
        copy(other, other).wait()
        return carry

    lax.fori_loop(1, devs, wait, 0)
    out[...] = held[...]


def return_part(parts, devs):
    return pl.pallas_call(
        return_kernel,
        out_shape=jax.ShapeDtypeStruct(parts.shape, parts.dtype),
        in_specs=[pl.BlockSpec(memory_space=VMEM)],
        out_specs=pl.BlockSpec(memory_space=VMEM),
        scratch_shapes=[
            VMEM(parts.shape, parts.dtype),
            pltpu.SemaphoreType.DMA((devs,)),
            pltpu.SemaphoreType.DMA((devs,)),
        ],
        compiler_params=pltpu.CompilerParams(
            collective_id=1, has_side_effects=True, vmem_limit_bytes=32 * 2**20
        ),
        name="returns",
    )(parts)


def place_kernel(owner, parts, out):
    caps = owner.shape[1]
    dev = lax.axis_index("dev")
    out[...] = jnp.zeros(out.shape, out.dtype)

    def one(e, carry):
        for k in range(caps):
            tile = owner[dev, k, e]
            at = pl.ds(pl.multiple_of(jnp.maximum(tile, 0) * TILE, TILE), TILE)
            out[0, :, at] += jnp.where(tile >= 0, parts[e, k].astype(out.dtype), 0.0)
        return carry

    lax.fori_loop(0, owner.shape[2], one, 0)


def place_part(owner, parts):
    return pl.pallas_call(
        place_kernel,
        out_shape=jax.ShapeDtypeStruct((1, parts.shape[2], NPHI), jnp.float32),
        in_specs=[pl.BlockSpec(memory_space=SMEM), pl.BlockSpec(memory_space=VMEM)],
        out_specs=pl.BlockSpec(memory_space=VMEM),
        compiler_params=pltpu.CompilerParams(vmem_limit_bytes=32 * 2**20),
        name="placing",
    )(owner, parts)


def local(
    field_mix,
    alm,
    legendre,
    order_ids,
    fetch_list,
    scan_tiles,
    block_tile,
    block_pix,
    noise_kernel,
    scan_weight,
):
    devs = lax.axis_size("dev")
    halves = lax.axis_size("half")
    order_slots, parts, fields, ells = alm.shape
    cycles = legendre.shape[2]
    owner = fetch_list.transpose(0, 2, 1)
    tiles = map_part(
        owner,
        order_ids.reshape(1, -1),
        field_mix,
        alm.reshape(order_slots * parts * fields, ells),
        legendre.transpose(0, 2, 1).reshape(order_slots * cycles, ells),
        devs,
        halves,
    )
    per_slot = scan_part(
        tiles.reshape((-1,) + tiles.shape[2:]),
        scan_tiles,
        block_tile,
        block_pix,
        noise_kernel,
        scan_weight,
    )
    returned = return_part(per_slot.reshape(tiles.shape), devs)
    return place_part(owner, returned)


def solution(mesh):
    return jax.shard_map(
        local,
        mesh=mesh,
        in_specs=(
            P("half", None),
            P("dev", None, "half", None),
            P("dev", None, None),
            P(),
            P(),
            P("dev", None),
            P("dev", None),
            P("dev", None),
            P("dev", None),
            P("dev"),
        ),
        out_specs=P("dev", "half", None),
        check_vma=False,
    )
```

```python
import functools
import math

import jax
import jax.numpy as jnp
from jax import lax
from jax.experimental import pallas as pl
from jax.experimental.pallas import tpu as pltpu
from jax.sharding import PartitionSpec as P

NPHI = 4096
TILE = 128
COLS = 256
VMEM = pltpu.VMEM
SMEM = pltpu.SMEM


MESH = pl.DeviceIdType.MESH
HIGHEST = lax.Precision.HIGHEST
SIDES = (((1,), (1,)), ((), ()))


def cos_sin(steps):
    quarter = NPHI // 2
    turn = (steps + quarter // 2) // quarter
    x = (steps - turn * quarter).astype(jnp.float32) * (math.pi / NPHI)
    y = x * x
    sin = x * (1 + y * (-1 / 6 + y * (1 / 120 + y * (-1 / 5040 + y / 362880))))
    cos = 1 + y * (-1 / 2 + y * (1 / 24 + y * (-1 / 720 + y * (1 / 40320 - y / 3628800))))
    odd = turn % 2 == 1
    cos_sign = jnp.where((turn == 1) | (turn == 2), -1.0, 1.0)
    sin_sign = jnp.where((turn == 2) | (turn == 3), -1.0, 1.0)
    return jnp.where(odd, sin, cos) * cos_sign, jnp.where(odd, cos, sin) * sin_sign


def meet(count, peer):
    barrier = pltpu.get_barrier_semaphore()

    def greet(i, carry):
        pl.semaphore_signal(barrier, inc=1, device_id=peer(i), device_id_type=MESH)
        return carry

    lax.fori_loop(1, count, greet, 0)
    return lambda: pl.semaphore_wait(barrier, count - 1)


def whole_kernel(
    owner, scan_tiles, block_tile, scan_weight, orders_hbm, mix_hbm, alm_hbm, legendre_hbm,
    pix_hbm, noise_hbm, out, orders, mix, alm, legendre, pix, noise, coeff_out, coeff_in, tiles,
    tiles_out, tiles_in, table, even, odd, weighted, parts, sums, back_out, back_in, loaded, sent,
    got, tile_sent, tile_got, back_sent, back_got,
):
    half, dev = lax.axis_index("half"), lax.axis_index("dev")
    halves, devs = lax.axis_size("half"), lax.axis_size("dev")
    everyone = halves * devs
    mine = half * devs + dev
    fields = mix.shape[0]
    caps = owner.shape[1]
    loads = [
        pltpu.make_async_copy(source, target, loaded.at[i])
        for i, (source, target) in enumerate(
            (
                (alm_hbm, alm),
                (legendre_hbm, legendre),
                (orders_hbm, orders),
                (mix_hbm, mix),
                (noise_hbm, noise),
                (pix_hbm, pix),
            )
        )
    ]
    for load in loads:
        load.start()
    cycles = coeff_out.shape[0]
    groups = coeff_out.shape[1]
    slots = alm.shape[0] // (2 * fields)

    def any_peer(i):
        other = lax.rem(mine + i, everyone)
        return {"half": other // devs, "dev": lax.rem(other, devs)}

    ready = meet(everyone, any_peer)
    for load in loads:
        load.wait()
    full = lax.dot_general(legendre[...], alm[...], SIDES, preferred_element_type=jnp.float32)
    lane = lax.broadcasted_iota(jnp.int32, (cycles, full.shape[1]), 1) // (2 * fields)
    own = jnp.zeros((cycles, full.shape[1]), jnp.float32)
    for s in range(slots):
        own = jnp.where(lane == s, full[s * cycles : (s + 1) * cycles], own)
    for q in range(groups):
        coeff_out[:, q, :] = own[:, q * TILE : (q + 1) * TILE]
    ready()

    def coeff_copy(target_half, target_dev, from_half, from_dev, n_out, n_in):
        return pltpu.make_async_remote_copy(
            src_ref=coeff_out.at[target_dev],
            dst_ref=coeff_in.at[from_half, from_dev],
            send_sem=sent.at[n_out],
            recv_sem=got.at[n_in],
            device_id={"half": target_half, "dev": target_dev},
            device_id_type=MESH,
        )

    def send_coeff(i, carry):
        other = lax.rem(mine + i, everyone)
        coeff_copy(other // devs, lax.rem(other, devs), half, dev, other, mine).start()
        return carry

    lax.fori_loop(1, everyone, send_coeff, 0)
    coeff_in[half, dev] = coeff_out[dev]

    total = orders.shape[1]
    per_group = slots // groups
    place = lax.broadcasted_iota(jnp.int32, (total, total), 1)
    place = place % devs * slots + place // devs % groups * per_group + place // (devs * groups)
    moves = (lax.broadcasted_iota(jnp.int32, (total, total), 0) == place).astype(jnp.float32)
    ids = jnp.dot(
        orders[...].astype(jnp.float32), moves, precision=HIGHEST,
        preferred_element_type=jnp.float32,
    )
    ids = jnp.round(ids).astype(jnp.int32)
    per_cycle = NPHI // TILE
    weight = jnp.where(ids == 0, 1.0, 2.0) / math.sqrt(2.0 * total)
    outer = lax.broadcasted_iota(jnp.int32, (per_cycle, total), 0) * (2 * TILE)
    inner = lax.broadcasted_iota(jnp.int32, (TILE, total), 0) * 2 + 1
    cos_out, sin_out = cos_sin(outer * ids % (2 * NPHI))
    basis = jnp.concatenate(cos_sin(inner * ids % (2 * NPHI)), axis=1)
    spread = []
    row_field = lax.broadcasted_iota(jnp.int32, (2 * fields, fields), 0) % fields
    pick_row = row_field == lax.broadcasted_iota(jnp.int32, (2 * fields, fields), 1)
    wide = (2 * fields, TILE)
    same = lax.broadcasted_iota(jnp.int32, wide, 0) // fields == (
        lax.broadcasted_iota(jnp.int32, wide, 1) // fields
    ) % 2
    for h in range(halves):
        lanes = (mix.shape[1], TILE)
        pick_lane = lax.broadcasted_iota(jnp.int32, lanes, 0) == (
            lax.broadcasted_iota(jnp.int32, lanes, 1) % fields + h * fields
        )
        rows = jnp.dot(
            pick_row.astype(jnp.float32), mix[...], precision=HIGHEST,
            preferred_element_type=jnp.float32,
        )
        rows = jnp.dot(
            rows, pick_lane.astype(jnp.float32), precision=HIGHEST,
            preferred_element_type=jnp.float32,
        )
        spread.append(jnp.where(same, rows, 0.0))

    def wait_coeff(i, carry):
        other = lax.rem(mine + i, everyone)
        copy = coeff_copy(
            other // devs, lax.rem(other, devs), other // devs, lax.rem(other, devs), other, other
        )
        copy.wait_recv()
        copy.wait_send()
        return carry

    scan_count, block_total = block_tile.shape
    length = pix.shape[1]
    block_len = length // block_total
    lags = noise.shape[1]
    per_block = block_len // COLS
    halo = lags // COLS
    window = 2 * lags + COLS
    rows = (length // COLS) * fields
    padded = (even, odd)
    edge = jnp.zeros((halo * fields, COLS), jnp.bfloat16)
    for ref in padded:
        ref[: halo * fields, :] = edge
        ref[halo * fields + rows :, :] = edge
    taps = noise[...].astype(jnp.bfloat16).astype(jnp.float32)
    lane = lax.broadcasted_iota(jnp.int32, taps.shape, 1)
    moved = jnp.where(lane == lags - 1, 0.0, pltpu.roll(taps, lags - 1, 1))
    turn = (
        lax.broadcasted_iota(jnp.int32, (TILE, TILE), 0)
        + lax.broadcasted_iota(jnp.int32, (TILE, TILE), 1)
        == TILE - 1
    ).astype(jnp.float32).astype(jnp.bfloat16)
    chunks = lags // TILE
    blank = jnp.zeros((scan_count, TILE), jnp.float32)
    turned = [
        jnp.dot(
            moved[:, c * TILE : (c + 1) * TILE].astype(jnp.bfloat16),
            turn,
            preferred_element_type=jnp.float32,
        )
        for c in range(chunks)
    ]
    band = jnp.concatenate([blank] + turned[::-1] + [taps] + [blank] * 2, axis=1)
    width = band.shape[1]
    top = width - COLS
    for n in range(scan_count):
        strip = pltpu.roll(
            jnp.broadcast_to(band[n : n + 1], (TILE, width)), 0, 1, stride=1, stride_axis=0
        ).astype(jnp.bfloat16)
        for q in range(window // TILE):
            start = top - q * TILE
            table[n, q * TILE : (q + 1) * TILE, :] = strip[:, start : start + COLS]

    lax.fori_loop(1, everyone, wait_coeff, 0)
    coeff = jnp.zeros((2 * fields, total), jnp.float32)
    for h in range(halves):
        block = jnp.concatenate([coeff_in[h, :, q, :] for q in range(groups)], axis=0)
        group = lax.broadcasted_iota(jnp.int32, block.shape, 1) // (2 * fields)
        block = jnp.concatenate(
            [jnp.where(group == s, block, 0.0) for s in range(per_group)], axis=0
        )
        coeff = coeff + lax.dot_general(
            spread[h], block, SIDES, precision=HIGHEST, preferred_element_type=jnp.float32
        )
    coeff = coeff * weight
    real, imag = coeff[:fields], coeff[fields:]
    turned = []
    for a in range(per_cycle):
        c, s = cos_out[a : a + 1], sin_out[a : a + 1]
        turned.append(jnp.concatenate([real * c - imag * s, -(real * s + imag * c)], axis=1))
    pixels = lax.dot_general(
        jnp.concatenate(turned, axis=0), basis, SIDES, precision=HIGHEST,
        preferred_element_type=jnp.float32,
    ).astype(jnp.bfloat16)
    for a in range(per_cycle):
        tiles[a] = pixels[a * fields : (a + 1) * fields]

    def tile_copy(target, source):
        return pltpu.make_async_remote_copy(
            src_ref=tiles_out.at[target],
            dst_ref=tiles_in.at[source],
            send_sem=tile_sent.at[target],
            recv_sem=tile_got.at[source],
            device_id={"half": half, "dev": target},
            device_id_type=MESH,
        )

    def send_tiles(i, carry):
        other = lax.rem(dev + i, devs)
        for k in range(caps):
            tiles_out[other, k] = tiles[jnp.maximum(owner[dev, k, other], 0)]
        tile_copy(other, dev).start()
        return carry

    lax.fori_loop(1, devs, send_tiles, 0)
    for k in range(caps):
        tiles_in[dev, k] = tiles[jnp.maximum(owner[dev, k, dev], 0)]

    def wait_tiles(i, carry):
        other = lax.rem(dev + i, devs)
        pltpu.make_async_remote_copy(
            src_ref=tiles_out.at[other],
            dst_ref=tiles_in.at[other],
            send_sem=tile_sent.at[other],
            recv_sem=tile_got.at[other],
            device_id={"half": half, "dev": other},
            device_id_type=MESH,
        ).wait()
        return carry

    slot_total = devs * caps
    select_shape = (slot_total, scan_count * block_total)
    slot_iota = lax.broadcasted_iota(jnp.int32, select_shape, 0)
    block_iota = lax.broadcasted_iota(jnp.int32, select_shape, 1)

    def mark(i, select):
        n, b = i // block_total, i % block_total
        slot = scan_tiles[n, block_tile[n, b]]
        return jnp.where((slot_iota == slot) & (block_iota == i), 1.0, select)

    select = lax.fori_loop(
        0, scan_count * block_total, mark, jnp.zeros(select_shape, jnp.float32)
    ).astype(jnp.bfloat16)
    lax.fori_loop(1, devs, wait_tiles, 0)


    below = lax.broadcasted_iota(jnp.int32, (TILE, block_len), 0).astype(jnp.float32).astype(
        jnp.bfloat16
    )

    def sample(n, b):
        slot = scan_tiles[n, block_tile[n, b]]
        tile = tiles_in[slot // caps, slot % caps].astype(jnp.float32)
        for c in range(block_len // TILE):
            at = pl.multiple_of(b * block_len + c * TILE, TILE)
            index = jnp.broadcast_to(pix[n : n + 1, pl.ds(at, TILE)], tile.shape)
            value = jnp.take_along_axis(
                tile, jnp.maximum(index, 0), axis=1, mode="promise_in_bounds"
            )
            value = jnp.where(index >= 0, value, 0.0).astype(jnp.bfloat16)
            row = pl.multiple_of((b * per_block + (c * TILE) // COLS + halo) * fields, 16)
            lane_at = (c * TILE) % COLS
            padded[n % 2][pl.ds(row, fields), lane_at : lane_at + TILE] = value

    def collect(n, b):
        at = pl.multiple_of(b * block_len, TILE)
        index = pix[n : n + 1, pl.ds(at, block_len)].astype(jnp.float32).astype(jnp.bfloat16)
        hot = jnp.where(
            below == index, jnp.ones((), jnp.bfloat16), jnp.zeros((), jnp.bfloat16)
        )
        row = jnp.concatenate(
            [
                weighted[pl.ds(pl.multiple_of((b * per_block + i) * fields, 16), fields), :]
                for i in range(per_block)
            ],
            axis=1,
        )
        part = lax.dot_general(
            row, hot, (((1,), (1,)), ((), ())), preferred_element_type=jnp.float32
        )
        parts[n * block_total + b] = part

    def together(step, group):
        def body(m, carry):
            for k in range(group):
                step(m * group + k)
            return carry

        lax.fori_loop(0, block_total // group, body, 0)

    group = 4
    while block_total % group:
        group //= 2
    together(lambda b: sample(0, b), group)
    for n in range(scan_count):
        pieces = [
            padded[n % 2][o * fields : o * fields + rows, :] for o in range(2 * halo + 1)
        ]
        filtered = jnp.dot(
            jnp.concatenate(pieces, axis=1), table[n], preferred_element_type=jnp.float32
        )
        weighted[...] = (scan_weight[n] * filtered).astype(jnp.bfloat16)

        def step(b):
            collect(n, b)
            if n + 1 < scan_count:
                sample(n + 1, b)

        together(step, group)
    for f in range(fields):
        exact = parts[:, f, :]
        high = exact.astype(jnp.bfloat16)
        low = (exact - high.astype(jnp.float32)).astype(jnp.bfloat16)
        sums[:, f, :] = jnp.dot(select, high, preferred_element_type=jnp.float32) + jnp.dot(
            select, low, preferred_element_type=jnp.float32
        )
    for e in range(devs):
        for k in range(caps):
            back_out[e, k] = sums[e * caps + k].astype(back_out.dtype)

    def back_copy(target, source):
        return pltpu.make_async_remote_copy(
            src_ref=back_out.at[target],
            dst_ref=back_in.at[source],
            send_sem=back_sent.at[target],
            recv_sem=back_got.at[source],
            device_id={"half": half, "dev": target},
            device_id_type=MESH,
        )

    def send_back(i, carry):
        back_copy(lax.rem(dev + i, devs), dev).start()
        return carry

    lax.fori_loop(1, devs, send_back, 0)
    back_in[dev] = back_out[dev]

    def wait_back(i, carry):
        other = lax.rem(dev + i, devs)
        back_copy(other, other).wait()
        return carry

    lax.fori_loop(1, devs, wait_back, 0)
    out[...] = back_in[...]


def whole_part(
    owner, scan_tiles, block_tile, scan_weight, orders, field_mix, alm, legendre, pix, noise, devs,
    halves,
):
    caps = owner.shape[1]
    fields = field_mix.shape[0]
    groups = alm.shape[0] // TILE
    cycles = legendre.shape[0] * 2 * fields // alm.shape[0]
    scan_count, lags = noise.shape
    length = pix.shape[1]
    blocks = scan_count * block_tile.shape[1]
    exchanged = (devs, caps, fields, TILE)
    halo_rows = (length + 2 * lags) // COLS * fields
    loads = (orders, field_mix, alm, legendre, pix, noise)
    return pl.pallas_call(
        whole_kernel,
        out_shape=jax.ShapeDtypeStruct(exchanged, jnp.bfloat16),
        in_specs=[pl.BlockSpec(memory_space=SMEM)] * 4
        + [pl.BlockSpec(memory_space=pltpu.HBM)] * len(loads),
        out_specs=pl.BlockSpec(memory_space=VMEM),
        scratch_shapes=[VMEM(x.shape, x.dtype) for x in loads]
        + [
            VMEM((cycles, groups, TILE), jnp.float32),
            VMEM((halves, devs, groups, TILE), jnp.float32),
            VMEM((NPHI // TILE, fields, TILE), jnp.bfloat16),
            VMEM(exchanged, jnp.bfloat16),
            VMEM(exchanged, jnp.bfloat16),
            VMEM((scan_count, 2 * lags + COLS, COLS), jnp.bfloat16),
            VMEM((halo_rows, COLS), jnp.bfloat16),
            VMEM((halo_rows, COLS), jnp.bfloat16),
            VMEM((length // COLS * fields, COLS), jnp.bfloat16),
            VMEM((blocks, fields, TILE), jnp.float32),
            VMEM((devs * caps, fields, TILE), jnp.float32),
            VMEM(exchanged, jnp.bfloat16),
            VMEM(exchanged, jnp.bfloat16),
            pltpu.SemaphoreType.DMA((len(loads),)),
            pltpu.SemaphoreType.DMA((halves * devs,)),
            pltpu.SemaphoreType.DMA((halves * devs,)),
            pltpu.SemaphoreType.DMA((devs,)),
            pltpu.SemaphoreType.DMA((devs,)),
            pltpu.SemaphoreType.DMA((devs,)),
            pltpu.SemaphoreType.DMA((devs,)),
        ],
        compiler_params=pltpu.CompilerParams(
            collective_id=0, has_side_effects=True, vmem_limit_bytes=60 * 2**20
        ),
        name="whole",
    )(owner, scan_tiles, block_tile, scan_weight, *loads)


def place_kernel(owner, parts, out):
    caps = owner.shape[1]
    dev = lax.axis_index("dev")
    out[...] = jnp.zeros(out.shape, out.dtype)

    def one(e, carry):
        for k in range(caps):
            tile = owner[dev, k, e]
            at = pl.ds(pl.multiple_of(jnp.maximum(tile, 0) * TILE, TILE), TILE)
            out[0, :, at] += jnp.where(tile >= 0, parts[e, k].astype(out.dtype), 0.0)
        return carry

    lax.fori_loop(0, owner.shape[2], one, 0)


def place_part(owner, parts):
    return pl.pallas_call(
        place_kernel,
        out_shape=jax.ShapeDtypeStruct((1, parts.shape[2], NPHI), jnp.float32),
        in_specs=[pl.BlockSpec(memory_space=SMEM), pl.BlockSpec(memory_space=VMEM)],
        out_specs=pl.BlockSpec(memory_space=VMEM),
        compiler_params=pltpu.CompilerParams(vmem_limit_bytes=32 * 2**20),
        name="placing",
    )(owner, parts)


def local(
    field_mix,
    alm,
    legendre,
    order_ids,
    fetch_list,
    scan_tiles,
    block_tile,
    block_pix,
    noise_kernel,
    scan_weight,
):
    devs = lax.axis_size("dev")
    halves = lax.axis_size("half")
    order_slots, parts, fields, ells = alm.shape
    cycles = legendre.shape[2]
    owner = fetch_list.transpose(0, 2, 1)
    returned = whole_part(
        owner,
        scan_tiles,
        block_tile,
        scan_weight,
        order_ids.reshape(1, -1),
        field_mix,
        alm.reshape(order_slots * parts * fields, ells),
        legendre.transpose(0, 2, 1).reshape(order_slots * cycles, ells),
        block_pix,
        noise_kernel,
        devs,
        halves,
    )
    return place_part(owner, returned)


def solution(mesh):
    return jax.shard_map(
        local,
        mesh=mesh,
        in_specs=(
            P("half", None),
            P("dev", None, "half", None),
            P("dev", None, None),
            P(),
            P(),
            P("dev", None),
            P("dev", None),
            P("dev", None),
            P("dev", None),
            P("dev"),
        ),
        out_specs=P("dev", "half", None),
        check_vma=False,
    )
```

```python
import functools
import math

import jax
import jax.numpy as jnp
from jax import lax
from jax.experimental import pallas as pl
from jax.experimental.pallas import tpu as pltpu
from jax.sharding import PartitionSpec as P

NPHI = 4096
TILE = 128
COLS = 256
VMEM = pltpu.VMEM
SMEM = pltpu.SMEM


MESH = pl.DeviceIdType.MESH
HIGHEST = lax.Precision.HIGHEST
SIDES = (((1,), (1,)), ((), ()))


def cos_sin(steps):
    quarter = NPHI // 2
    turn = (steps + quarter // 2) // quarter
    x = (steps - turn * quarter).astype(jnp.float32) * (math.pi / NPHI)
    y = x * x
    sin = x * (1 + y * (-1 / 6 + y * (1 / 120 + y * (-1 / 5040 + y / 362880))))
    cos = 1 + y * (-1 / 2 + y * (1 / 24 + y * (-1 / 720 + y * (1 / 40320 - y / 3628800))))
    odd = turn % 2 == 1
    cos_sign = jnp.where((turn == 1) | (turn == 2), -1.0, 1.0)
    sin_sign = jnp.where((turn == 2) | (turn == 3), -1.0, 1.0)
    return jnp.where(odd, sin, cos) * cos_sign, jnp.where(odd, cos, sin) * sin_sign


def meet(count, peer):
    barrier = pltpu.get_barrier_semaphore()

    def greet(i, carry):
        pl.semaphore_signal(barrier, inc=1, device_id=peer(i), device_id_type=MESH)
        return carry

    lax.fori_loop(1, count, greet, 0)
    return lambda: pl.semaphore_wait(barrier, count - 1)


def whole_kernel(
    owner, scan_tiles, block_tile, scan_weight, orders_hbm, mix_hbm, alm_hbm, legendre_hbm,
    pix_hbm, noise_hbm, out, orders, mix, alm, legendre, pix, noise, coeff_out, coeff_in, tiles,
    tiles_out, tiles_in, table, points, padded, weighted, parts, sums, own_tiles, back_out,
    back_in, loaded, sent, got, tile_sent, tile_got, back_sent, back_got,
):
    half, dev = lax.axis_index("half"), lax.axis_index("dev")
    halves, devs = lax.axis_size("half"), lax.axis_size("dev")
    everyone = halves * devs
    mine = half * devs + dev
    fields = mix.shape[0]
    caps = owner.shape[1]
    loads = [
        pltpu.make_async_copy(source, target, loaded.at[i])
        for i, (source, target) in enumerate(
            (
                (alm_hbm, alm),
                (legendre_hbm, legendre),
                (orders_hbm, orders),
                (mix_hbm, mix),
                (noise_hbm, noise),
                (pix_hbm, pix),
            )
        )
    ]
    for load in loads:
        load.start()
    cycles = coeff_out.shape[0]
    groups = coeff_out.shape[1]
    slots = alm.shape[0] // (2 * fields)

    def any_peer(i):
        other = lax.rem(mine + i, everyone)
        return {"half": other // devs, "dev": lax.rem(other, devs)}

    ready = meet(everyone, any_peer)
    for load in loads:
        load.wait()
    full = lax.dot_general(legendre[...], alm[...], SIDES, preferred_element_type=jnp.float32)
    lane = lax.broadcasted_iota(jnp.int32, (cycles, full.shape[1]), 1) // (2 * fields)
    own = jnp.zeros((cycles, full.shape[1]), jnp.float32)
    for s in range(slots):
        own = jnp.where(lane == s, full[s * cycles : (s + 1) * cycles], own)
    for q in range(groups):
        coeff_out[:, q, :] = own[:, q * TILE : (q + 1) * TILE]
    ready()

    def coeff_copy(target_half, target_dev, from_half, from_dev, n_out, n_in):
        return pltpu.make_async_remote_copy(
            src_ref=coeff_out.at[target_dev],
            dst_ref=coeff_in.at[from_half, from_dev],
            send_sem=sent.at[n_out],
            recv_sem=got.at[n_in],
            device_id={"half": target_half, "dev": target_dev},
            device_id_type=MESH,
        )

    def send_coeff(i, carry):
        other = lax.rem(mine + i, everyone)
        coeff_copy(other // devs, lax.rem(other, devs), half, dev, other, mine).start()
        return carry

    lax.fori_loop(1, everyone, send_coeff, 0)
    coeff_in[half, dev] = coeff_out[dev]

    total = orders.shape[1]
    per_group = slots // groups
    place = lax.broadcasted_iota(jnp.int32, (total, total), 1)
    place = place % devs * slots + place // devs % groups * per_group + place // (devs * groups)
    moves = (lax.broadcasted_iota(jnp.int32, (total, total), 0) == place).astype(jnp.float32)
    ids = jnp.dot(
        orders[...].astype(jnp.float32), moves, precision=HIGHEST,
        preferred_element_type=jnp.float32,
    )
    ids = jnp.round(ids).astype(jnp.int32)
    per_cycle = NPHI // TILE
    weight = jnp.where(ids == 0, 1.0, 2.0) / math.sqrt(2.0 * total)
    outer = lax.broadcasted_iota(jnp.int32, (per_cycle, total), 0) * (2 * TILE)
    inner = lax.broadcasted_iota(jnp.int32, (TILE, total), 0) * 2 + 1
    cos_out, sin_out = cos_sin(outer * ids % (2 * NPHI))
    basis = jnp.concatenate(cos_sin(inner * ids % (2 * NPHI)), axis=1)
    spread = []
    row_field = lax.broadcasted_iota(jnp.int32, (2 * fields, fields), 0) % fields
    pick_row = row_field == lax.broadcasted_iota(jnp.int32, (2 * fields, fields), 1)
    wide = (2 * fields, TILE)
    same = lax.broadcasted_iota(jnp.int32, wide, 0) // fields == (
        lax.broadcasted_iota(jnp.int32, wide, 1) // fields
    ) % 2
    for h in range(halves):
        lanes = (mix.shape[1], TILE)
        pick_lane = lax.broadcasted_iota(jnp.int32, lanes, 0) == (
            lax.broadcasted_iota(jnp.int32, lanes, 1) % fields + h * fields
        )
        rows = jnp.dot(
            pick_row.astype(jnp.float32), mix[...], precision=HIGHEST,
            preferred_element_type=jnp.float32,
        )
        rows = jnp.dot(
            rows, pick_lane.astype(jnp.float32), precision=HIGHEST,
            preferred_element_type=jnp.float32,
        )
        spread.append(jnp.where(same, rows, 0.0))

    def wait_coeff(i, carry):
        other = lax.rem(mine + i, everyone)
        copy = coeff_copy(
            other // devs, lax.rem(other, devs), other // devs, lax.rem(other, devs), other, other
        )
        copy.wait_recv()
        copy.wait_send()
        return carry

    scan_count, block_total = block_tile.shape
    length = pix.shape[1]
    block_len = length // block_total
    lags = noise.shape[1]
    per_block = block_len // COLS
    halo = lags // COLS
    window = 2 * lags + COLS
    rows = (length // COLS) * fields
    edge = jnp.zeros((halo * fields, COLS), jnp.bfloat16)
    padded[: halo * fields, :] = edge
    padded[halo * fields + rows :, :] = edge
    for n in range(scan_count):

        def cut(b, carry):
            at = pl.multiple_of(b * block_len, TILE)
            points[n * block_total + b] = pix[n : n + 1, pl.ds(at, block_len)]
            return carry

        lax.fori_loop(0, block_total, cut, 0, unroll=4)
    taps = noise[...].astype(jnp.bfloat16).astype(jnp.float32)
    lane = lax.broadcasted_iota(jnp.int32, taps.shape, 1)
    moved = jnp.where(lane == lags - 1, 0.0, pltpu.roll(taps, lags - 1, 1))
    turn = (
        lax.broadcasted_iota(jnp.int32, (TILE, TILE), 0)
        + lax.broadcasted_iota(jnp.int32, (TILE, TILE), 1)
        == TILE - 1
    ).astype(jnp.float32).astype(jnp.bfloat16)
    chunks = lags // TILE
    blank = jnp.zeros((scan_count, TILE), jnp.float32)
    turned = [
        jnp.dot(
            moved[:, c * TILE : (c + 1) * TILE].astype(jnp.bfloat16),
            turn,
            preferred_element_type=jnp.float32,
        )
        for c in range(chunks)
    ]
    band = jnp.concatenate([blank] + turned[::-1] + [taps] + [blank] * 2, axis=1)
    width = band.shape[1]
    top = width - COLS
    for n in range(scan_count):
        strip = pltpu.roll(
            jnp.broadcast_to(band[n : n + 1], (TILE, width)), 0, 1, stride=1, stride_axis=0
        ).astype(jnp.bfloat16)
        for q in range(window // TILE):
            start = top - q * TILE
            table[n, q * TILE : (q + 1) * TILE, :] = strip[:, start : start + COLS]

    lax.fori_loop(1, everyone, wait_coeff, 0)
    coeff = jnp.zeros((2 * fields, total), jnp.float32)
    for h in range(halves):
        block = jnp.concatenate([coeff_in[h, :, q, :] for q in range(groups)], axis=0)
        group = lax.broadcasted_iota(jnp.int32, block.shape, 1) // (2 * fields)
        block = jnp.concatenate(
            [jnp.where(group == s, block, 0.0) for s in range(per_group)], axis=0
        )
        coeff = coeff + lax.dot_general(
            spread[h], block, SIDES, precision=HIGHEST, preferred_element_type=jnp.float32
        )
    coeff = coeff * weight
    real, imag = coeff[:fields], coeff[fields:]
    turned = []
    for a in range(per_cycle):
        c, s = cos_out[a : a + 1], sin_out[a : a + 1]
        turned.append(jnp.concatenate([real * c - imag * s, -(real * s + imag * c)], axis=1))
    pixels = lax.dot_general(
        jnp.concatenate(turned, axis=0), basis, SIDES, precision=HIGHEST,
        preferred_element_type=jnp.float32,
    ).astype(jnp.bfloat16)
    for a in range(per_cycle):
        tiles[a] = pixels[a * fields : (a + 1) * fields]

    def tile_copy(target, source):
        return pltpu.make_async_remote_copy(
            src_ref=tiles_out.at[target],
            dst_ref=tiles_in.at[source],
            send_sem=tile_sent.at[target],
            recv_sem=tile_got.at[source],
            device_id={"half": half, "dev": target},
            device_id_type=MESH,
        )

    def send_tiles(i, carry):
        other = lax.rem(dev + i, devs)
        for k in range(caps):
            tiles_out[other, k] = tiles[jnp.maximum(owner[dev, k, other], 0)]
        tile_copy(other, dev).start()
        return carry

    lax.fori_loop(1, devs, send_tiles, 0)
    for k in range(caps):
        tiles_in[dev, k] = tiles[jnp.maximum(owner[dev, k, dev], 0)]

    def wait_tiles(i, carry):
        other = lax.rem(dev + i, devs)
        pltpu.make_async_remote_copy(
            src_ref=tiles_out.at[other],
            dst_ref=tiles_in.at[other],
            send_sem=tile_sent.at[other],
            recv_sem=tile_got.at[other],
            device_id={"half": half, "dev": other},
            device_id_type=MESH,
        ).wait()
        return carry

    slot_total = devs * caps
    select_shape = (slot_total, scan_count * block_total)
    slot_iota = lax.broadcasted_iota(jnp.int32, select_shape, 0)
    block_iota = lax.broadcasted_iota(jnp.int32, select_shape, 1)

    def mark(i, select):
        n, b = i // block_total, i % block_total
        slot = scan_tiles[n, block_tile[n, b]]
        return jnp.where((slot_iota == slot) & (block_iota == i), 1.0, select)

    select = lax.fori_loop(
        0, scan_count * block_total, mark, jnp.zeros(select_shape, jnp.float32)
    ).astype(jnp.bfloat16)
    place_shape = (per_cycle, slot_total)
    tile_iota = lax.broadcasted_iota(jnp.int32, place_shape, 0)
    place_iota = lax.broadcasted_iota(jnp.int32, place_shape, 1)

    def mark_tile(i, placing):
        tile = owner[dev, i % caps, i // caps]
        return jnp.where((tile_iota == tile) & (place_iota == i), 1.0, placing)

    placing = lax.fori_loop(
        0, slot_total, mark_tile, jnp.zeros(place_shape, jnp.float32)
    ).astype(jnp.bfloat16)
    lax.fori_loop(1, devs, wait_tiles, 0)


    below = lax.broadcasted_iota(jnp.int32, (TILE, block_len), 0).astype(jnp.float32).astype(
        jnp.bfloat16
    )

    def sample(n, b):
        slot = scan_tiles[n, block_tile[n, b]]
        tile = tiles_in[slot // caps, slot % caps].astype(jnp.float32)
        for c in range(block_len // TILE):
            index = points[n * block_total + b, :, c * TILE : (c + 1) * TILE]
            index = jnp.broadcast_to(index, tile.shape)
            value = jnp.take_along_axis(
                tile, jnp.maximum(index, 0), axis=1, mode="promise_in_bounds"
            )
            value = jnp.where(index >= 0, value, 0.0).astype(jnp.bfloat16)
            row = pl.multiple_of((b * per_block + (c * TILE) // COLS + halo) * fields, 16)
            lane_at = (c * TILE) % COLS
            padded[pl.ds(row, fields), lane_at : lane_at + TILE] = value

    def collect(n, b):
        index = points[n * block_total + b].astype(jnp.float32).astype(jnp.bfloat16)
        hot = jnp.where(
            below == index, jnp.ones((), jnp.bfloat16), jnp.zeros((), jnp.bfloat16)
        )
        row = jnp.concatenate(
            [
                weighted[pl.ds(pl.multiple_of((b * per_block + i) * fields, 16), fields), :]
                for i in range(per_block)
            ],
            axis=1,
        )
        part = lax.dot_general(
            row, hot, (((1,), (1,)), ((), ())), preferred_element_type=jnp.float32
        )
        parts[n * block_total + b] = part

    def together(step, group):
        def body(m, carry):
            for k in range(group):
                step(m * group + k)
            return carry

        lax.fori_loop(0, block_total // group, body, 0)

    group = 16
    while block_total % group:
        group //= 2
    together(lambda b: sample(0, b), group)

    def one_scan(n, carry):
        pieces = [padded[o * fields : o * fields + rows, :] for o in range(2 * halo + 1)]
        filtered = jnp.dot(
            jnp.concatenate(pieces, axis=1), table[n], preferred_element_type=jnp.float32
        )
        weighted[...] = (scan_weight[n] * filtered).astype(jnp.bfloat16)

        def step(b):
            collect(n, b)
            sample(lax.min(n + 1, scan_count - 1), b)

        together(step, group)
        return carry

    lax.fori_loop(0, scan_count, one_scan, 0)
    for f in range(fields):
        exact = parts[:, f, :]
        high = exact.astype(jnp.bfloat16)
        low = (exact - high.astype(jnp.float32)).astype(jnp.bfloat16)
        sums[:, f, :] = jnp.dot(select, high, preferred_element_type=jnp.float32) + jnp.dot(
            select, low, preferred_element_type=jnp.float32
        )
    for e in range(devs):
        for k in range(caps):
            back_out[e, k] = sums[e * caps + k].astype(back_out.dtype)

    def back_copy(target, source):
        return pltpu.make_async_remote_copy(
            src_ref=back_out.at[target],
            dst_ref=back_in.at[source],
            send_sem=back_sent.at[target],
            recv_sem=back_got.at[source],
            device_id={"half": half, "dev": target},
            device_id_type=MESH,
        )

    def send_back(i, carry):
        back_copy(lax.rem(dev + i, devs), dev).start()
        return carry

    lax.fori_loop(1, devs, send_back, 0)
    back_in[dev] = back_out[dev]

    def wait_back(i, carry):
        other = lax.rem(dev + i, devs)
        back_copy(other, other).wait()
        return carry

    lax.fori_loop(1, devs, wait_back, 0)
    for e in range(devs):
        for k in range(caps):
            sums[e * caps + k] = back_in[e, k].astype(jnp.float32)
    for f in range(fields):
        own_tiles[:, f, :] = jnp.dot(
            placing, sums[:, f, :].astype(jnp.bfloat16), preferred_element_type=jnp.float32
        )
    for a in range(per_cycle):
        out[0, :, a * TILE : (a + 1) * TILE] = own_tiles[a]


def whole_part(
    owner, scan_tiles, block_tile, scan_weight, orders, field_mix, alm, legendre, pix, noise, devs,
    halves,
):
    caps = owner.shape[1]
    fields = field_mix.shape[0]
    groups = alm.shape[0] // TILE
    cycles = legendre.shape[0] * 2 * fields // alm.shape[0]
    scan_count, lags = noise.shape
    length = pix.shape[1]
    blocks = scan_count * block_tile.shape[1]
    exchanged = (devs, caps, fields, TILE)
    halo_rows = (length + 2 * lags) // COLS * fields
    loads = (orders, field_mix, alm, legendre, pix, noise)
    return pl.pallas_call(
        whole_kernel,
        out_shape=jax.ShapeDtypeStruct((1, fields, NPHI), jnp.float32),
        in_specs=[pl.BlockSpec(memory_space=SMEM)] * 4
        + [pl.BlockSpec(memory_space=pltpu.HBM)] * len(loads),
        out_specs=pl.BlockSpec(memory_space=VMEM),
        scratch_shapes=[VMEM(x.shape, x.dtype) for x in loads]
        + [
            VMEM((cycles, groups, TILE), jnp.float32),
            VMEM((halves, devs, groups, TILE), jnp.float32),
            VMEM((NPHI // TILE, fields, TILE), jnp.bfloat16),
            VMEM(exchanged, jnp.bfloat16),
            VMEM(exchanged, jnp.bfloat16),
            VMEM((scan_count, 2 * lags + COLS, COLS), jnp.bfloat16),
            VMEM((blocks, 1, length // block_tile.shape[1]), jnp.int32),
            VMEM((halo_rows, COLS), jnp.bfloat16),
            VMEM((length // COLS * fields, COLS), jnp.bfloat16),
            VMEM((blocks, fields, TILE), jnp.float32),
            VMEM((devs * caps, fields, TILE), jnp.float32),
            VMEM((NPHI // TILE, fields, TILE), jnp.float32),
            VMEM(exchanged, jnp.bfloat16),
            VMEM(exchanged, jnp.bfloat16),
            pltpu.SemaphoreType.DMA((len(loads),)),
            pltpu.SemaphoreType.DMA((halves * devs,)),
            pltpu.SemaphoreType.DMA((halves * devs,)),
            pltpu.SemaphoreType.DMA((devs,)),
            pltpu.SemaphoreType.DMA((devs,)),
            pltpu.SemaphoreType.DMA((devs,)),
            pltpu.SemaphoreType.DMA((devs,)),
        ],
        compiler_params=pltpu.CompilerParams(
            collective_id=0, has_side_effects=True, vmem_limit_bytes=60 * 2**20
        ),
        name="whole",
    )(owner, scan_tiles, block_tile, scan_weight, *loads)


def local(
    field_mix,
    alm,
    legendre,
    order_ids,
    fetch_list,
    scan_tiles,
    block_tile,
    block_pix,
    noise_kernel,
    scan_weight,
):
    devs = lax.axis_size("dev")
    halves = lax.axis_size("half")
    order_slots, parts, fields, ells = alm.shape
    cycles = legendre.shape[2]
    owner = fetch_list.transpose(0, 2, 1)
    return whole_part(
        owner,
        scan_tiles,
        block_tile,
        scan_weight,
        order_ids.reshape(1, -1),
        field_mix,
        alm.reshape(order_slots * parts * fields, ells),
        legendre.transpose(0, 2, 1).reshape(order_slots * cycles, ells),
        block_pix,
        noise_kernel,
        devs,
        halves,
    )


def solution(mesh):
    return jax.shard_map(
        local,
        mesh=mesh,
        in_specs=(
            P("half", None),
            P("dev", None, "half", None),
            P("dev", None, None),
            P(),
            P(),
            P("dev", None),
            P("dev", None),
            P("dev", None),
            P("dev", None),
            P("dev"),
        ),
        out_specs=P("dev", "half", None),
        check_vma=False,
    )
```

```python
import functools
import math

import jax
import jax.numpy as jnp
from jax import lax
from jax.experimental import pallas as pl
from jax.experimental.pallas import tpu as pltpu
from jax.sharding import PartitionSpec as P

NPHI = 4096
TILE = 128
COLS = 256
ROWS = 8
VMEM = pltpu.VMEM
SMEM = pltpu.SMEM


MESH = pl.DeviceIdType.MESH
HIGHEST = lax.Precision.HIGHEST
SIDES = (((1,), (1,)), ((), ()))


def cos_sin(steps):
    quarter = NPHI // 2
    turn = (steps + quarter // 2) // quarter
    x = (steps - turn * quarter).astype(jnp.float32) * (math.pi / NPHI)
    y = x * x
    sin = x * (1 + y * (-1 / 6 + y * (1 / 120 + y * (-1 / 5040 + y / 362880))))
    cos = 1 + y * (-1 / 2 + y * (1 / 24 + y * (-1 / 720 + y * (1 / 40320 - y / 3628800))))
    odd = turn % 2 == 1
    cos_sign = jnp.where((turn == 1) | (turn == 2), -1.0, 1.0)
    sin_sign = jnp.where((turn == 2) | (turn == 3), -1.0, 1.0)
    return jnp.where(odd, sin, cos) * cos_sign, jnp.where(odd, cos, sin) * sin_sign


def meet(count, peer):
    barrier = pltpu.get_barrier_semaphore()

    def greet(i, carry):
        pl.semaphore_signal(barrier, inc=1, device_id=peer(i), device_id_type=MESH)
        return carry

    lax.fori_loop(1, count, greet, 0)
    return lambda: pl.semaphore_wait(barrier, count - 1)


def whole_kernel(
    owner, scan_tiles, block_tile, scan_weight, orders_hbm, mix_hbm, alm_hbm, legendre_hbm,
    pix_hbm, noise_hbm, out, orders, mix, alm, legendre, pix, noise, coeff_out, coeff_in, tiles,
    tiles_out, tiles_in, table, points, padded, weighted, parts, sums, back_out,
    back_in, loaded, sent, got, tile_sent, tile_got, back_sent, back_got,
):
    half, dev = lax.axis_index("half"), lax.axis_index("dev")
    halves, devs = lax.axis_size("half"), lax.axis_size("dev")
    everyone = halves * devs
    mine = half * devs + dev
    fields = mix.shape[0]
    caps = owner.shape[1]
    loads = [
        pltpu.make_async_copy(source, target, loaded.at[i])
        for i, (source, target) in enumerate(
            (
                (alm_hbm, alm),
                (legendre_hbm, legendre),
                (orders_hbm, orders),
                (mix_hbm, mix),
                (noise_hbm, noise),
                (pix_hbm, pix),
            )
        )
    ]
    for load in loads:
        load.start()
    cycles = coeff_out.shape[0]
    groups = coeff_out.shape[1]
    slots = alm.shape[0] // (2 * fields)

    def any_peer(i):
        other = lax.rem(mine + i, everyone)
        return {"half": other // devs, "dev": lax.rem(other, devs)}

    ready = meet(everyone, any_peer)
    for load in loads:
        load.wait()
    full = lax.dot_general(legendre[...], alm[...], SIDES, preferred_element_type=jnp.float32)
    lane = lax.broadcasted_iota(jnp.int32, (cycles, full.shape[1]), 1) // (2 * fields)
    own = jnp.zeros((cycles, full.shape[1]), jnp.float32)
    for s in range(slots):
        own = jnp.where(lane == s, full[s * cycles : (s + 1) * cycles], own)
    for q in range(groups):
        coeff_out[:, q, :] = own[:, q * TILE : (q + 1) * TILE]
    ready()

    def coeff_copy(target_half, target_dev, from_half, from_dev, n_out, n_in):
        return pltpu.make_async_remote_copy(
            src_ref=coeff_out.at[target_dev],
            dst_ref=coeff_in.at[from_half, from_dev],
            send_sem=sent.at[n_out],
            recv_sem=got.at[n_in],
            device_id={"half": target_half, "dev": target_dev},
            device_id_type=MESH,
        )

    def send_coeff(i, carry):
        other = lax.rem(mine + i, everyone)
        coeff_copy(other // devs, lax.rem(other, devs), half, dev, other, mine).start()
        return carry

    lax.fori_loop(1, everyone, send_coeff, 0)
    coeff_in[half, dev] = coeff_out[dev]

    total = orders.shape[1]
    per_group = slots // groups
    place = lax.broadcasted_iota(jnp.int32, (total, total), 1)
    place = place % devs * slots + place // devs % groups * per_group + place // (devs * groups)
    moves = (lax.broadcasted_iota(jnp.int32, (total, total), 0) == place).astype(jnp.float32)
    ids = jnp.dot(
        orders[...].astype(jnp.float32), moves, precision=HIGHEST,
        preferred_element_type=jnp.float32,
    )
    ids = jnp.round(ids).astype(jnp.int32)
    per_cycle = NPHI // TILE
    weight = jnp.where(ids == 0, 1.0, 2.0)
    outer = lax.broadcasted_iota(jnp.int32, (per_cycle, total), 0) * (2 * TILE)
    inner = lax.broadcasted_iota(jnp.int32, (TILE, total), 0) * 2 + 1
    cos_out, sin_out = cos_sin(outer * ids % (2 * NPHI))
    basis = jnp.concatenate(cos_sin(inner * ids % (2 * NPHI)), axis=1)
    spread = []
    row_field = lax.broadcasted_iota(jnp.int32, (2 * fields, fields), 0) % fields
    pick_row = row_field == lax.broadcasted_iota(jnp.int32, (2 * fields, fields), 1)
    wide = (2 * fields, TILE)
    same = lax.broadcasted_iota(jnp.int32, wide, 0) // fields == (
        lax.broadcasted_iota(jnp.int32, wide, 1) // fields
    ) % 2
    for h in range(halves):
        lanes = (mix.shape[1], TILE)
        pick_lane = lax.broadcasted_iota(jnp.int32, lanes, 0) == (
            lax.broadcasted_iota(jnp.int32, lanes, 1) % fields + h * fields
        )
        rows = jnp.dot(
            pick_row.astype(jnp.float32), mix[...], precision=HIGHEST,
            preferred_element_type=jnp.float32,
        )
        rows = jnp.dot(
            rows, pick_lane.astype(jnp.float32), precision=HIGHEST,
            preferred_element_type=jnp.float32,
        )
        spread.append(jnp.where(same, rows, 0.0))

    def wait_coeff(i, carry):
        other = lax.rem(mine + i, everyone)
        there, at = other // devs, lax.rem(other, devs)
        coeff_copy(there, at, there, at, other, other).wait_recv()
        return carry

    scan_count, block_total = block_tile.shape
    length = pix.shape[1]
    block_len = length // block_total
    lags = noise.shape[1]
    per_block = block_len // COLS
    halo = lags // COLS
    window = 2 * lags + COLS
    rows = (length // COLS) * fields
    for n in range(scan_count):

        def cut(b, carry):
            at = pl.multiple_of(b * block_len, TILE)
            points[n * block_total + b] = pix[n : n + 1, pl.ds(at, block_len)]
            return carry

        lax.fori_loop(0, block_total, cut, 0, unroll=4)
    lax.fori_loop(1, everyone, wait_coeff, 0)
    coeff = jnp.zeros((2 * fields, total), jnp.float32)
    for h in range(halves):
        block = jnp.concatenate([coeff_in[h, :, q, :] for q in range(groups)], axis=0)
        group = lax.broadcasted_iota(jnp.int32, block.shape, 1) // (2 * fields)
        block = jnp.concatenate(
            [jnp.where(group == s, block, 0.0) for s in range(per_group)], axis=0
        )
        coeff = coeff + lax.dot_general(
            spread[h], block, SIDES, precision=HIGHEST, preferred_element_type=jnp.float32
        )
    coeff = coeff * weight
    real, imag = coeff[:fields], coeff[fields:]
    turned = []
    for a in range(per_cycle):
        c, s = cos_out[a : a + 1], sin_out[a : a + 1]
        turned.append(jnp.concatenate([real * c - imag * s, -(real * s + imag * c)], axis=1))
    pixels = lax.dot_general(
        jnp.concatenate(turned, axis=0), basis, SIDES, precision=HIGHEST,
        preferred_element_type=jnp.float32,
    ).astype(jnp.bfloat16)
    for a in range(per_cycle):
        tiles[a] = pixels[a * fields : (a + 1) * fields]

    def tile_copy(target, source):
        return pltpu.make_async_remote_copy(
            src_ref=tiles_out.at[target],
            dst_ref=tiles_in.at[source],
            send_sem=tile_sent.at[target],
            recv_sem=tile_got.at[source],
            device_id={"half": half, "dev": target},
            device_id_type=MESH,
        )

    def send_tiles(i, carry):
        other = lax.rem(dev + i, devs)
        for k in range(caps):
            tiles_out[other, k] = tiles[jnp.maximum(owner[dev, k, other], 0)]
        tile_copy(other, dev).start()
        return carry

    lax.fori_loop(1, devs, send_tiles, 0)
    for k in range(caps):
        tiles_in[dev, k] = tiles[jnp.maximum(owner[dev, k, dev], 0)]

    def wait_tiles(i, carry):
        other = lax.rem(dev + i, devs)
        tile_copy(other, other).wait_recv()
        return carry

    edge = jnp.zeros((halo * fields, COLS), jnp.bfloat16)
    padded[: halo * fields, :] = edge
    padded[halo * fields + rows :, :] = edge
    taps = noise[...].astype(jnp.bfloat16).astype(jnp.float32)
    lane = lax.broadcasted_iota(jnp.int32, taps.shape, 1)
    moved = jnp.where(lane == lags - 1, 0.0, pltpu.roll(taps, lags - 1, 1))
    turn = (
        lax.broadcasted_iota(jnp.int32, (TILE, TILE), 0)
        + lax.broadcasted_iota(jnp.int32, (TILE, TILE), 1)
        == TILE - 1
    ).astype(jnp.float32).astype(jnp.bfloat16)
    chunks = lags // TILE
    blank = jnp.zeros((scan_count, TILE), jnp.float32)
    turned = [
        jnp.dot(
            moved[:, c * TILE : (c + 1) * TILE].astype(jnp.bfloat16),
            turn,
            preferred_element_type=jnp.float32,
        )
        for c in range(chunks)
    ]
    band = jnp.concatenate([blank] + turned[::-1] + [taps] + [blank] * 2, axis=1)
    width = band.shape[1]
    top = width - COLS
    for n in range(scan_count):
        strip = pltpu.roll(
            jnp.broadcast_to(band[n : n + 1], (TILE, width)), 0, 1, stride=1, stride_axis=0
        ).astype(jnp.bfloat16)
        for q in range(window // TILE):
            start = top - q * TILE
            table[n, q * TILE : (q + 1) * TILE, :] = strip[:, start : start + COLS]

    slot_total = devs * caps
    select_shape = (slot_total, scan_count * block_total)
    slot_iota = lax.broadcasted_iota(jnp.int32, select_shape, 0)
    block_iota = lax.broadcasted_iota(jnp.int32, select_shape, 1)

    def mark(i, select):
        n, b = i // block_total, i % block_total
        slot = scan_tiles[n, block_tile[n, b]]
        return jnp.where((slot_iota == slot) & (block_iota == i), 1.0, select)

    select = lax.fori_loop(
        0, scan_count * block_total, mark, jnp.zeros(select_shape, jnp.float32)
    ).astype(jnp.bfloat16)
    lax.fori_loop(1, devs, wait_tiles, 0)


    below = lax.broadcasted_iota(jnp.int32, (TILE, block_len), 0).astype(jnp.float32).astype(
        jnp.bfloat16
    )

    def sample(n, b):
        slot = scan_tiles[n, block_tile[n, b]]
        tile = tiles_in[slot // caps, slot % caps].astype(jnp.float32)
        for c in range(block_len // TILE):
            index = points[n * block_total + b, :, c * TILE : (c + 1) * TILE]
            index = jnp.broadcast_to(index, tile.shape)
            value = jnp.take_along_axis(
                tile, jnp.maximum(index, 0), axis=1, mode="promise_in_bounds"
            )
            value = jnp.where(index >= 0, value, 0.0).astype(jnp.bfloat16)
            row = pl.multiple_of((b * per_block + (c * TILE) // COLS + halo) * fields, 16)
            lane_at = (c * TILE) % COLS
            padded[pl.ds(row, fields), lane_at : lane_at + TILE] = value

    def collect(n, b):
        index = points[n * block_total + b].astype(jnp.float32).astype(jnp.bfloat16)
        hot = jnp.where(
            below == index, jnp.ones((), jnp.bfloat16), jnp.zeros((), jnp.bfloat16)
        )
        row = jnp.concatenate(
            [
                weighted[pl.ds(pl.multiple_of((b * per_block + i) * fields, 16), fields), :]
                for i in range(per_block)
            ],
            axis=1,
        )
        part = lax.dot_general(
            row, hot, (((1,), (1,)), ((), ())), preferred_element_type=jnp.float32
        )
        parts[n * block_total + b] = part

    def together(step, group):
        def body(m, carry):
            for k in range(group):
                step(m * group + k)
            return carry

        lax.fori_loop(0, block_total // group, body, 0)

    group = 32
    while block_total % group:
        group //= 2
    together(lambda b: sample(0, b), group)

    def one_scan(n, carry):
        pieces = [padded[o * fields : o * fields + rows, :] for o in range(2 * halo + 1)]
        filtered = jnp.dot(
            jnp.concatenate(pieces, axis=1), table[n], preferred_element_type=jnp.float32
        )
        weighted[...] = (scan_weight[n] * filtered).astype(jnp.bfloat16)

        def step(b):
            collect(n, b)
            sample(lax.min(n + 1, scan_count - 1), b)

        together(step, group)
        return carry

    lax.fori_loop(0, scan_count, one_scan, 0)
    for f in range(fields):
        exact = parts[:, f, :]
        high = exact.astype(jnp.bfloat16)
        low = (exact - high.astype(jnp.float32)).astype(jnp.bfloat16)
        sums[:, f, :] = jnp.dot(select, high, preferred_element_type=jnp.float32) + jnp.dot(
            select, low, preferred_element_type=jnp.float32
        )
    for e in range(devs):
        for k in range(caps):
            back_out[e, k] = sums[e * caps + k].astype(back_out.dtype)

    def back_copy(target, source):
        return pltpu.make_async_remote_copy(
            src_ref=back_out.at[target],
            dst_ref=back_in.at[source],
            send_sem=back_sent.at[target],
            recv_sem=back_got.at[source],
            device_id={"half": half, "dev": target},
            device_id_type=MESH,
        )

    def send_back(i, carry):
        back_copy(lax.rem(dev + i, devs), dev).start()
        return carry

    lax.fori_loop(1, devs, send_back, 0)
    back_in[dev] = back_out[dev]

    def wait_back(i, carry):
        other = lax.rem(dev + i, devs)
        back_copy(other, other).wait()
        return carry

    place_shape = (per_cycle, slot_total)
    tile_iota = lax.broadcasted_iota(jnp.int32, place_shape, 0)
    place_iota = lax.broadcasted_iota(jnp.int32, place_shape, 1)

    def mark_tile(i, placing):
        tile = owner[dev, i % caps, i // caps]
        return jnp.where((tile_iota == tile) & (place_iota == i), 1.0, placing)

    placing = lax.fori_loop(
        0, slot_total, mark_tile, jnp.zeros(place_shape, jnp.float32)
    ).astype(jnp.bfloat16)

    def drain_coeff(i, carry):
        other = lax.rem(mine + i, everyone)
        there, at = other // devs, lax.rem(other, devs)
        coeff_copy(there, at, there, at, other, other).wait_send()
        return carry

    lax.fori_loop(1, everyone, drain_coeff, 0)

    def drain_tiles(i, carry):
        other = lax.rem(dev + i, devs)
        tile_copy(other, other).wait_send()
        return carry

    lax.fori_loop(1, devs, drain_tiles, 0)
    lax.fori_loop(1, devs, wait_back, 0)
    for e in range(devs):
        for k in range(caps):
            sums[e * caps + k] = back_in[e, k].astype(jnp.float32)
    for f in range(fields):
        out[f // ROWS, :, f % ROWS, :] = jnp.dot(
            placing, sums[:, f, :].astype(jnp.bfloat16), preferred_element_type=jnp.float32
        )


def whole_part(
    owner, scan_tiles, block_tile, scan_weight, orders, field_mix, alm, legendre, pix, noise, devs,
    halves,
):
    caps = owner.shape[1]
    fields = field_mix.shape[0]
    groups = alm.shape[0] // TILE
    cycles = legendre.shape[0] * 2 * fields // alm.shape[0]
    scan_count, lags = noise.shape
    length = pix.shape[1]
    blocks = scan_count * block_tile.shape[1]
    exchanged = (devs, caps, fields, TILE)
    halo_rows = (length + 2 * lags) // COLS * fields
    loads = (orders, field_mix, alm, legendre, pix, noise)
    return pl.pallas_call(
        whole_kernel,
        out_shape=jax.ShapeDtypeStruct(
            (fields // ROWS, NPHI // TILE, ROWS, TILE), jnp.float32
        ),
        in_specs=[pl.BlockSpec(memory_space=SMEM)] * 4
        + [pl.BlockSpec(memory_space=pltpu.HBM)] * len(loads),
        out_specs=pl.BlockSpec(memory_space=VMEM),
        scratch_shapes=[VMEM(x.shape, x.dtype) for x in loads]
        + [
            VMEM((cycles, groups, TILE), jnp.float32),
            VMEM((halves, devs, groups, TILE), jnp.float32),
            VMEM((NPHI // TILE, fields, TILE), jnp.bfloat16),
            VMEM(exchanged, jnp.bfloat16),
            VMEM(exchanged, jnp.bfloat16),
            VMEM((scan_count, 2 * lags + COLS, COLS), jnp.bfloat16),
            VMEM((blocks, 1, length // block_tile.shape[1]), jnp.int32),
            VMEM((halo_rows, COLS), jnp.bfloat16),
            VMEM((length // COLS * fields, COLS), jnp.bfloat16),
            VMEM((blocks, fields, TILE), jnp.float32),
            VMEM((devs * caps, fields, TILE), jnp.float32),
            VMEM(exchanged, jnp.bfloat16),
            VMEM(exchanged, jnp.bfloat16),
            pltpu.SemaphoreType.DMA((len(loads),)),
            pltpu.SemaphoreType.DMA((halves * devs,)),
            pltpu.SemaphoreType.DMA((halves * devs,)),
            pltpu.SemaphoreType.DMA((devs,)),
            pltpu.SemaphoreType.DMA((devs,)),
            pltpu.SemaphoreType.DMA((devs,)),
            pltpu.SemaphoreType.DMA((devs,)),
        ],
        compiler_params=pltpu.CompilerParams(
            collective_id=0, has_side_effects=True, vmem_limit_bytes=60 * 2**20
        ),
        name="whole",
    )(owner, scan_tiles, block_tile, scan_weight, *loads)


def local(
    field_mix,
    alm,
    legendre,
    order_ids,
    fetch_list,
    scan_tiles,
    block_tile,
    block_pix,
    noise_kernel,
    scan_weight,
):
    devs = lax.axis_size("dev")
    halves = lax.axis_size("half")
    order_slots, parts, fields, ells = alm.shape
    cycles = legendre.shape[2]
    owner = fetch_list.transpose(0, 2, 1)
    binned = whole_part(
        owner,
        scan_tiles,
        block_tile,
        scan_weight,
        order_ids.reshape(1, -1),
        field_mix,
        alm.reshape(order_slots * parts * fields, ells),
        legendre.transpose(0, 2, 1).reshape(order_slots * cycles, ells),
        block_pix,
        noise_kernel,
        devs,
        halves,
    )
    binned = binned.transpose(0, 2, 1, 3).reshape(1, fields, NPHI)
    return binned * (1.0 / math.sqrt(2.0 * order_ids.shape[0]))


def solution(mesh):
    return jax.shard_map(
        local,
        mesh=mesh,
        in_specs=(
            P("half", None),
            P("dev", None, "half", None),
            P("dev", None, None),
            P(),
            P(),
            P("dev", None),
            P("dev", None),
            P("dev", None),
            P("dev", None),
            P("dev"),
        ),
        out_specs=P("dev", "half", None),
        check_vma=False,
    )
```

```python
import functools
import math

import jax
import jax.numpy as jnp
from jax import lax
from jax.experimental import pallas as pl
from jax.experimental.pallas import tpu as pltpu
from jax.sharding import PartitionSpec as P

NPHI = 4096
TILE = 128
COLS = 256
VMEM = pltpu.VMEM
SMEM = pltpu.SMEM


MESH = pl.DeviceIdType.MESH
HIGHEST = lax.Precision.HIGHEST
SIDES = (((1,), (1,)), ((), ()))


def cos_sin(steps):
    quarter = NPHI // 2
    turn = (steps + quarter // 2) // quarter
    x = (steps - turn * quarter).astype(jnp.float32) * (math.pi / NPHI)
    y = x * x
    sin = x * (1 + y * (-1 / 6 + y * (1 / 120 + y * (-1 / 5040 + y / 362880))))
    cos = 1 + y * (-1 / 2 + y * (1 / 24 + y * (-1 / 720 + y * (1 / 40320 - y / 3628800))))
    odd = turn % 2 == 1
    cos_sign = jnp.where((turn == 1) | (turn == 2), -1.0, 1.0)
    sin_sign = jnp.where((turn == 2) | (turn == 3), -1.0, 1.0)
    return jnp.where(odd, sin, cos) * cos_sign, jnp.where(odd, cos, sin) * sin_sign


def meet(count, peer):
    barrier = pltpu.get_barrier_semaphore()

    def greet(i, carry):
        pl.semaphore_signal(barrier, inc=1, device_id=peer(i), device_id_type=MESH)
        return carry

    lax.fori_loop(1, count, greet, 0)
    return lambda: pl.semaphore_wait(barrier, count - 1)


def whole_kernel(
    owner, scan_tiles, block_tile, scan_weight, orders_hbm, mix_hbm, alm_hbm, legendre_hbm,
    pix_hbm, noise_hbm, out, orders, mix, alm, legendre, pix, noise, coeff_out, coeff_in, tiles,
    tiles_out, tiles_in, table, points, padded, weighted, parts, sums, own_tiles, back_out,
    back_in, loaded, sent, got, tile_sent, tile_got, back_sent, back_got,
):
    half, dev = lax.axis_index("half"), lax.axis_index("dev")
    halves, devs = lax.axis_size("half"), lax.axis_size("dev")
    everyone = halves * devs
    mine = half * devs + dev
    fields = mix.shape[0]
    caps = owner.shape[1]
    loads = [
        pltpu.make_async_copy(source, target, loaded.at[i])
        for i, (source, target) in enumerate(
            (
                (alm_hbm, alm),
                (legendre_hbm, legendre),
                (orders_hbm, orders),
                (mix_hbm, mix),
                (noise_hbm, noise),
                (pix_hbm, pix),
            )
        )
    ]
    for load in loads:
        load.start()
    cycles = coeff_out.shape[0]
    groups = coeff_out.shape[1]
    slots = alm.shape[0] // (2 * fields)

    def any_peer(i):
        other = lax.rem(mine + i, everyone)
        return {"half": other // devs, "dev": lax.rem(other, devs)}

    ready = meet(everyone, any_peer)
    for load in loads:
        load.wait()
    full = lax.dot_general(legendre[...], alm[...], SIDES, preferred_element_type=jnp.float32)
    lane = lax.broadcasted_iota(jnp.int32, (cycles, full.shape[1]), 1) // (2 * fields)
    own = jnp.zeros((cycles, full.shape[1]), jnp.float32)
    for s in range(slots):
        own = jnp.where(lane == s, full[s * cycles : (s + 1) * cycles], own)
    for q in range(groups):
        coeff_out[:, q, :] = own[:, q * TILE : (q + 1) * TILE]
    ready()

    def coeff_copy(target_half, target_dev, from_half, from_dev, n_out, n_in):
        return pltpu.make_async_remote_copy(
            src_ref=coeff_out.at[target_dev],
            dst_ref=coeff_in.at[from_half, from_dev],
            send_sem=sent.at[n_out],
            recv_sem=got.at[n_in],
            device_id={"half": target_half, "dev": target_dev},
            device_id_type=MESH,
        )

    def send_coeff(i, carry):
        other = lax.rem(mine + i, everyone)
        coeff_copy(other // devs, lax.rem(other, devs), half, dev, other, mine).start()
        return carry

    lax.fori_loop(1, everyone, send_coeff, 0)
    coeff_in[half, dev] = coeff_out[dev]

    total = orders.shape[1]
    per_group = slots // groups
    place = lax.broadcasted_iota(jnp.int32, (total, total), 1)
    place = place % devs * slots + place // devs % groups * per_group + place // (devs * groups)
    moves = (lax.broadcasted_iota(jnp.int32, (total, total), 0) == place).astype(jnp.float32)
    ids = jnp.dot(
        orders[...].astype(jnp.float32), moves, precision=HIGHEST,
        preferred_element_type=jnp.float32,
    )
    ids = jnp.round(ids).astype(jnp.int32)
    per_cycle = NPHI // TILE
    weight = jnp.where(ids == 0, 1.0, 2.0) / math.sqrt(2.0 * total)
    outer = lax.broadcasted_iota(jnp.int32, (per_cycle, total), 0) * (2 * TILE)
    inner = lax.broadcasted_iota(jnp.int32, (TILE, total), 0) * 2 + 1
    cos_out, sin_out = cos_sin(outer * ids % (2 * NPHI))
    basis = jnp.concatenate(cos_sin(inner * ids % (2 * NPHI)), axis=1)
    spread = []
    row_field = lax.broadcasted_iota(jnp.int32, (2 * fields, fields), 0) % fields
    pick_row = row_field == lax.broadcasted_iota(jnp.int32, (2 * fields, fields), 1)
    wide = (2 * fields, TILE)
    same = lax.broadcasted_iota(jnp.int32, wide, 0) // fields == (
        lax.broadcasted_iota(jnp.int32, wide, 1) // fields
    ) % 2
    for h in range(halves):
        lanes = (mix.shape[1], TILE)
        pick_lane = lax.broadcasted_iota(jnp.int32, lanes, 0) == (
            lax.broadcasted_iota(jnp.int32, lanes, 1) % fields + h * fields
        )
        rows = jnp.dot(
            pick_row.astype(jnp.float32), mix[...], precision=HIGHEST,
            preferred_element_type=jnp.float32,
        )
        rows = jnp.dot(
            rows, pick_lane.astype(jnp.float32), precision=HIGHEST,
            preferred_element_type=jnp.float32,
        )
        spread.append(jnp.where(same, rows, 0.0))

    def wait_coeff(i, carry):
        other = lax.rem(mine + i, everyone)
        there, at = other // devs, lax.rem(other, devs)
        coeff_copy(there, at, there, at, other, other).wait_recv()
        return carry

    scan_count, block_total = block_tile.shape
    length = pix.shape[1]
    block_len = length // block_total
    lags = noise.shape[1]
    per_block = block_len // COLS
    halo = lags // COLS
    window = 2 * lags + COLS
    rows = (length // COLS) * fields
    edge = jnp.zeros((halo * fields, COLS), jnp.bfloat16)
    padded[: halo * fields, :] = edge
    padded[halo * fields + rows :, :] = edge
    for n in range(scan_count):

        def cut(b, carry):
            at = pl.multiple_of(b * block_len, TILE)
            points[n * block_total + b] = pix[n : n + 1, pl.ds(at, block_len)]
            return carry

        lax.fori_loop(0, block_total, cut, 0, unroll=4)
    taps = noise[...].astype(jnp.bfloat16).astype(jnp.float32)
    lane = lax.broadcasted_iota(jnp.int32, taps.shape, 1)
    moved = jnp.where(lane == lags - 1, 0.0, pltpu.roll(taps, lags - 1, 1))
    turn = (
        lax.broadcasted_iota(jnp.int32, (TILE, TILE), 0)
        + lax.broadcasted_iota(jnp.int32, (TILE, TILE), 1)
        == TILE - 1
    ).astype(jnp.float32).astype(jnp.bfloat16)
    chunks = lags // TILE
    blank = jnp.zeros((scan_count, TILE), jnp.float32)
    turned = [
        jnp.dot(
            moved[:, c * TILE : (c + 1) * TILE].astype(jnp.bfloat16),
            turn,
            preferred_element_type=jnp.float32,
        )
        for c in range(chunks)
    ]
    band = jnp.concatenate([blank] + turned[::-1] + [taps] + [blank] * 2, axis=1)
    width = band.shape[1]
    top = width - COLS
    for n in range(scan_count):
        strip = pltpu.roll(
            jnp.broadcast_to(band[n : n + 1], (TILE, width)), 0, 1, stride=1, stride_axis=0
        ).astype(jnp.bfloat16)
        for q in range(window // TILE):
            start = top - q * TILE
            table[n, q * TILE : (q + 1) * TILE, :] = strip[:, start : start + COLS]

    lax.fori_loop(1, everyone, wait_coeff, 0)
    coeff = jnp.zeros((2 * fields, total), jnp.float32)
    for h in range(halves):
        block = jnp.concatenate([coeff_in[h, :, q, :] for q in range(groups)], axis=0)
        group = lax.broadcasted_iota(jnp.int32, block.shape, 1) // (2 * fields)
        block = jnp.concatenate(
            [jnp.where(group == s, block, 0.0) for s in range(per_group)], axis=0
        )
        coeff = coeff + lax.dot_general(
            spread[h], block, SIDES, precision=HIGHEST, preferred_element_type=jnp.float32
        )
    coeff = coeff * weight
    real, imag = coeff[:fields], coeff[fields:]
    turned = []
    for a in range(per_cycle):
        c, s = cos_out[a : a + 1], sin_out[a : a + 1]
        turned.append(jnp.concatenate([real * c - imag * s, -(real * s + imag * c)], axis=1))
    pixels = lax.dot_general(
        jnp.concatenate(turned, axis=0), basis, SIDES, precision=HIGHEST,
        preferred_element_type=jnp.float32,
    ).astype(jnp.bfloat16)
    for a in range(per_cycle):
        tiles[a] = pixels[a * fields : (a + 1) * fields]

    def tile_copy(target, source):
        return pltpu.make_async_remote_copy(
            src_ref=tiles_out.at[target],
            dst_ref=tiles_in.at[source],
            send_sem=tile_sent.at[target],
            recv_sem=tile_got.at[source],
            device_id={"half": half, "dev": target},
            device_id_type=MESH,
        )

    def send_tiles(i, carry):
        other = lax.rem(dev + i, devs)
        for k in range(caps):
            tiles_out[other, k] = tiles[jnp.maximum(owner[dev, k, other], 0)]
        tile_copy(other, dev).start()
        return carry

    lax.fori_loop(1, devs, send_tiles, 0)
    for k in range(caps):
        tiles_in[dev, k] = tiles[jnp.maximum(owner[dev, k, dev], 0)]

    def wait_tiles(i, carry):
        other = lax.rem(dev + i, devs)
        tile_copy(other, other).wait_recv()
        return carry

    slot_total = devs * caps
    select_shape = (slot_total, scan_count * block_total)
    slot_iota = lax.broadcasted_iota(jnp.int32, select_shape, 0)
    block_iota = lax.broadcasted_iota(jnp.int32, select_shape, 1)

    def mark(i, select):
        n, b = i // block_total, i % block_total
        slot = scan_tiles[n, block_tile[n, b]]
        return jnp.where((slot_iota == slot) & (block_iota == i), 1.0, select)

    select = lax.fori_loop(
        0, scan_count * block_total, mark, jnp.zeros(select_shape, jnp.float32), unroll=8
    ).astype(jnp.bfloat16)
    lax.fori_loop(1, devs, wait_tiles, 0)


    below = lax.broadcasted_iota(jnp.int32, (TILE, block_len), 0).astype(jnp.float32).astype(
        jnp.bfloat16
    )

    def sample(n, b):
        slot = scan_tiles[n, block_tile[n, b]]
        tile = tiles_in[slot // caps, slot % caps].astype(jnp.float32)
        for c in range(block_len // TILE):
            index = points[n * block_total + b, :, c * TILE : (c + 1) * TILE]
            index = jnp.broadcast_to(index, tile.shape)
            value = jnp.take_along_axis(
                tile, jnp.maximum(index, 0), axis=1, mode="promise_in_bounds"
            )
            value = jnp.where(index >= 0, value, 0.0).astype(jnp.bfloat16)
            row = pl.multiple_of((b * per_block + (c * TILE) // COLS + halo) * fields, 16)
            lane_at = (c * TILE) % COLS
            padded[pl.ds(row, fields), lane_at : lane_at + TILE] = value

    def collect(n, b):
        index = points[n * block_total + b].astype(jnp.float32).astype(jnp.bfloat16)
        hot = jnp.where(
            below == index, jnp.ones((), jnp.bfloat16), jnp.zeros((), jnp.bfloat16)
        )
        row = jnp.concatenate(
            [
                weighted[pl.ds(pl.multiple_of((b * per_block + i) * fields, 16), fields), :]
                for i in range(per_block)
            ],
            axis=1,
        )
        part = lax.dot_general(
            row, hot, (((1,), (1,)), ((), ())), preferred_element_type=jnp.float32
        )
        parts[n * block_total + b] = part

    def together(step, group):
        def body(m, carry):
            for k in range(group):
                step(m * group + k)
            return carry

        lax.fori_loop(0, block_total // group, body, 0)

    group = 16
    while block_total % group:
        group //= 2
    together(lambda b: sample(0, b), group)

    def one_scan(n, carry):
        pieces = [padded[o * fields : o * fields + rows, :] for o in range(2 * halo + 1)]
        filtered = jnp.dot(
            jnp.concatenate(pieces, axis=1), table[n], preferred_element_type=jnp.float32
        )
        weighted[...] = (scan_weight[n] * filtered).astype(jnp.bfloat16)

        def step(b):
            collect(n, b)
            sample(lax.min(n + 1, scan_count - 1), b)

        together(step, group)
        return carry

    lax.fori_loop(0, scan_count, one_scan, 0)
    for f in range(fields):
        exact = parts[:, f, :]
        high = exact.astype(jnp.bfloat16)
        low = (exact - high.astype(jnp.float32)).astype(jnp.bfloat16)
        sums[:, f, :] = jnp.dot(select, high, preferred_element_type=jnp.float32) + jnp.dot(
            select, low, preferred_element_type=jnp.float32
        )
    for e in range(devs):
        for k in range(caps):
            back_out[e, k] = sums[e * caps + k].astype(back_out.dtype)

    def back_copy(target, source):
        return pltpu.make_async_remote_copy(
            src_ref=back_out.at[target],
            dst_ref=back_in.at[source],
            send_sem=back_sent.at[target],
            recv_sem=back_got.at[source],
            device_id={"half": half, "dev": target},
            device_id_type=MESH,
        )

    def send_back(i, carry):
        back_copy(lax.rem(dev + i, devs), dev).start()
        return carry

    lax.fori_loop(1, devs, send_back, 0)
    back_in[dev] = back_out[dev]

    def wait_back(i, carry):
        other = lax.rem(dev + i, devs)
        back_copy(other, other).wait()
        return carry

    place_shape = (per_cycle, slot_total)
    tile_iota = lax.broadcasted_iota(jnp.int32, place_shape, 0)
    place_iota = lax.broadcasted_iota(jnp.int32, place_shape, 1)

    def mark_tile(i, placing):
        tile = owner[dev, i % caps, i // caps]
        return jnp.where((tile_iota == tile) & (place_iota == i), 1.0, placing)

    placing = lax.fori_loop(
        0, slot_total, mark_tile, jnp.zeros(place_shape, jnp.float32), unroll=8
    ).astype(jnp.bfloat16)

    def drain_coeff(i, carry):
        other = lax.rem(mine + i, everyone)
        there, at = other // devs, lax.rem(other, devs)
        coeff_copy(there, at, there, at, other, other).wait_send()
        return carry

    lax.fori_loop(1, everyone, drain_coeff, 0)

    def drain_tiles(i, carry):
        other = lax.rem(dev + i, devs)
        tile_copy(other, other).wait_send()
        return carry

    lax.fori_loop(1, devs, drain_tiles, 0)
    lax.fori_loop(1, devs, wait_back, 0)
    for e in range(devs):
        for k in range(caps):
            sums[e * caps + k] = back_in[e, k].astype(jnp.float32)
    for f in range(fields):
        own_tiles[:, f, :] = jnp.dot(
            placing, sums[:, f, :].astype(jnp.bfloat16), preferred_element_type=jnp.float32
        )
    for a in range(per_cycle):
        out[0, :, a * TILE : (a + 1) * TILE] = own_tiles[a]


def whole_part(
    owner, scan_tiles, block_tile, scan_weight, orders, field_mix, alm, legendre, pix, noise, devs,
    halves,
):
    caps = owner.shape[1]
    fields = field_mix.shape[0]
    groups = alm.shape[0] // TILE
    cycles = legendre.shape[0] * 2 * fields // alm.shape[0]
    scan_count, lags = noise.shape
    length = pix.shape[1]
    blocks = scan_count * block_tile.shape[1]
    exchanged = (devs, caps, fields, TILE)
    halo_rows = (length + 2 * lags) // COLS * fields
    loads = (orders, field_mix, alm, legendre, pix, noise)
    return pl.pallas_call(
        whole_kernel,
        out_shape=jax.ShapeDtypeStruct((1, fields, NPHI), jnp.float32),
        in_specs=[pl.BlockSpec(memory_space=SMEM)] * 4
        + [pl.BlockSpec(memory_space=pltpu.HBM)] * len(loads),
        out_specs=pl.BlockSpec(memory_space=VMEM),
        scratch_shapes=[VMEM(x.shape, x.dtype) for x in loads]
        + [
            VMEM((cycles, groups, TILE), jnp.float32),
            VMEM((halves, devs, groups, TILE), jnp.float32),
            VMEM((NPHI // TILE, fields, TILE), jnp.bfloat16),
            VMEM(exchanged, jnp.bfloat16),
            VMEM(exchanged, jnp.bfloat16),
            VMEM((scan_count, 2 * lags + COLS, COLS), jnp.bfloat16),
            VMEM((blocks, 1, length // block_tile.shape[1]), jnp.int32),
            VMEM((halo_rows, COLS), jnp.bfloat16),
            VMEM((length // COLS * fields, COLS), jnp.bfloat16),
            VMEM((blocks, fields, TILE), jnp.float32),
            VMEM((devs * caps, fields, TILE), jnp.float32),
            VMEM((NPHI // TILE, fields, TILE), jnp.float32),
            VMEM(exchanged, jnp.bfloat16),
            VMEM(exchanged, jnp.bfloat16),
            pltpu.SemaphoreType.DMA((len(loads),)),
            pltpu.SemaphoreType.DMA((halves * devs,)),
            pltpu.SemaphoreType.DMA((halves * devs,)),
            pltpu.SemaphoreType.DMA((devs,)),
            pltpu.SemaphoreType.DMA((devs,)),
            pltpu.SemaphoreType.DMA((devs,)),
            pltpu.SemaphoreType.DMA((devs,)),
        ],
        compiler_params=pltpu.CompilerParams(
            collective_id=0, has_side_effects=True, vmem_limit_bytes=60 * 2**20
        ),
        name="whole",
    )(owner, scan_tiles, block_tile, scan_weight, *loads)


def local(
    field_mix,
    alm,
    legendre,
    order_ids,
    fetch_list,
    scan_tiles,
    block_tile,
    block_pix,
    noise_kernel,
    scan_weight,
):
    devs = lax.axis_size("dev")
    halves = lax.axis_size("half")
    order_slots, parts, fields, ells = alm.shape
    cycles = legendre.shape[2]
    owner = fetch_list.transpose(0, 2, 1)
    return whole_part(
        owner,
        scan_tiles,
        block_tile,
        scan_weight,
        order_ids.reshape(1, -1),
        field_mix,
        alm.reshape(order_slots * parts * fields, ells),
        legendre.transpose(0, 2, 1).reshape(order_slots * cycles, ells),
        block_pix,
        noise_kernel,
        devs,
        halves,
    )


def solution(mesh):
    return jax.shard_map(
        local,
        mesh=mesh,
        in_specs=(
            P("half", None),
            P("dev", None, "half", None),
            P("dev", None, None),
            P(),
            P(),
            P("dev", None),
            P("dev", None),
            P("dev", None),
            P("dev", None),
            P("dev"),
        ),
        out_specs=P("dev", "half", None),
        check_vma=False,
    )
```
